128 devices in a mesh: dp: 4 (over y), seq: 4 (over x), expert: 8 (over z, core).
Axes of the slice: x: 4, y: 4, z: 4, core: 2. Of those that a mesh axis runs over, the one named last changes fastest.
Arguments:
- queries: bfloat16 [32, 512, 2048], P(('dp', 'expert'), 'seq'), may hold values from -135 to 135
- keys: bfloat16 [32, 512, 2048], P(('dp', 'expert'), 'seq'), may hold values from -5 to 5
- values: bfloat16 [32, 512, 2048], P(('dp', 'expert'), 'seq'), may hold values from -6 to 6
- resid: bfloat16 [32, 512, 2048], P(('dp', 'expert'), 'seq'), may hold values from -20 to 20
- cotangent: bfloat16 [32, 512, 2048], P(('dp', 'expert'), 'seq'), may hold values from -0.3125 to 0.3125
- zone_ids: int32 [32, 512, 1], P(('dp', 'expert'), 'seq'), may hold values from 0 to 31; in each aligned block of 128 rows (0 to 127, 128 to 255, ..., all dimensions but the last counted through in order) at most 10 rows name the same one
- norm_gain: float32 [2048], replicated, may hold values from 0.1 to 1.9
- w_in: bfloat16 [32, 2048, 4096], P(('seq', 'expert'), None, 'dp'), may hold values from -0.125 to 0.125
- w_out: bfloat16 [32, 4096, 2048], P(('seq', 'expert'), 'dp'), may hold values from -0.09375 to 0.09375
Outputs:
- layer_out: bfloat16 [32, 512, 2048], P(('dp', 'expert'), 'seq')
- grad_w_in: bfloat16 [32, 2048, 4096], P(('seq', 'expert'), None, 'dp')
- grad_w_out: bfloat16 [32, 4096, 2048], P(('seq', 'expert'), 'dp')
The draws below stay inside these ranges and needn't reach their ends.
Inputs may be any that keep to these rules, and one draw needn't show every extreme that they name: `zone_ids`: among the tokens of one device at most 10 name the same expert, and that count is reached.
All inputs are finite; a program needn't handle non-finite values.
Results may differ from the reference program's by a relative error of at most 0.0085.
Values may be sent and summed in bfloat16 or wider, within the bound.
No kernel may reach another device: no remote copies, remote signals or barrier semaphores. Data moves between devices by JAX's collectives and lax.ppermute only.
A program may use at most 128 MiB of HBM per device.

```python
import math
import jax
import jax.numpy as jnp
import numpy as np
from jax import lax

D = 2048
HEADS = 16
H = 4096
WIN_LEN = 512
HEAD_DIM = 128
SHARD_LEN = 128
WINDOWS = 32
TOKENS = 16384
EXPERTS = 32
CAP = 10
SLOTS = 1280


def common_plan(key):
    base_keys = jnp.clip(jax.random.normal(jax.random.fold_in(key, 101), (WINDOWS, WIN_LEN, D), jnp.float32), -5.0, 5.0)
    return base_keys


def draw_keys(key, part):
    base_keys = common_plan(key)
    return base_keys.astype(jnp.bfloat16)


def draw_queries(key, part):
    result = jnp.clip(jax.random.normal(jax.random.fold_in(key, 201), (WINDOWS, WIN_LEN, D), jnp.float32), -5.0, 5.0)
    return result.astype(jnp.bfloat16)


def draw_resid(key, part):
    extent = (WINDOWS, WIN_LEN, D)
    row_scale = jnp.exp(jax.random.uniform(jax.random.fold_in(key, 302), (WINDOWS, WIN_LEN, 1), jnp.float32, math.log(0.2), math.log(2.0)))
    col_scale = jnp.exp(jax.random.uniform(jax.random.fold_in(key, 303), (1, 1, D), jnp.float32, math.log(0.2), math.log(2.0)))
    jitter = jnp.clip(jax.random.normal(jax.random.fold_in(key, 301), extent, jnp.float32), -5.0, 5.0)
    return (jitter * row_scale * col_scale).astype(jnp.bfloat16)


def block_levels(key, shape, split, low, largest):
    level, own = 1.0, jax.random.fold_in(key, 6)
    for axis_at, blocks in split:
        steps = jnp.exp(jax.random.uniform(jax.random.fold_in(own, axis_at), (blocks,), jnp.float32, low / len(split), largest / len(split)))
        level = level * jnp.repeat(steps, shape[axis_at] // blocks).reshape([-1 if axis == axis_at else 1 for axis in range(len(shape))])
    return level


def routed_block(stream_key, own, number, rows, number_of, top, limit, lean):
    order = jax.random.permutation(stream_key, number_of)
    heavy_load, ordinary = shares(number_of, rows * top, limit, lean, True), shares(number_of, rows * top, limit, lean, False)
    places = jnp.arange(number_of)

    def named(lengths, offset_by):
        used = int((lengths > 0).sum())
        fixed = max(1, used // 4)
        passed = fixed + (places - fixed + offset_by * (used - fixed)) % max(1, number_of - fixed)
        return jnp.zeros((number_of,), jnp.int32).at[order[jnp.where(places < fixed, places, passed)]].set(jnp.asarray(lengths, jnp.int32))

    lengths = jnp.where(number % 4 == 0, named(heavy_load, number // 4), named(ordinary, number - number // 4 - 1))
    mixed = jax.random.permutation(jax.random.fold_in(own, 3), number_of)
    source_of, taker = mixed[0:number_of // 2 * 2:2], mixed[1:number_of // 2 * 2:2]
    slack = jnp.minimum(lengths[source_of] - 1, limit - lengths[taker]) // 2
    slack = jnp.where((source_of == order[0]) | (taker == order[0]) | (lengths[taker] == 0), 0, jnp.maximum(slack, 0))
    passed = jax.random.randint(jax.random.fold_in(own, 4), (number_of // 2,), 0, 1 << 20) % (slack + 1)
    lengths = lengths.at[source_of].add(-passed).at[taker].add(passed)
    labels = jnp.searchsorted(jnp.cumsum(lengths), jnp.arange(rows * top), side="right").astype(jnp.int32)
    table = labels.reshape(top, rows).T
    table = table[jax.random.permutation(jax.random.fold_in(own, 1), rows)]
    offset_by = jax.random.randint(jax.random.fold_in(own, 2), (rows, 1), 0, top)
    return jnp.take_along_axis(table, (jnp.arange(top)[None, :] + offset_by) % top, axis=1)


def shares(count, total, reach, lean, full):
    loads = [(1 << 20) // math.isqrt(standing ** lean) + 1 for standing in range(1, count + 1)]
    largest = reach if full else min(reach, max(-(-total // count), total * loads[0] // sum(loads)))
    least = 1 if total - largest >= count - 1 else 0
    holding, spare = [largest] + [least] * (count - 1), total - largest - least * (count - 1)
    while spare > 0:
        candidates = [i for i in range(1, count) if holding[i] < largest] or [i for i in range(1, count) if holding[i] < reach]
        whole, left = sum([loads[i] for i in candidates]), spare
        for i in candidates:
            addition = min(reach - holding[i], max(1, left * loads[i] // whole), spare)
            holding[i] = holding[i] + addition
            spare = spare - addition
    return np.array(holding)


def gaussian(rng, shape, width, reach, split=(), kind=jnp.bfloat16):
    values = jax.random.normal(rng, shape, jnp.float32) * width
    if len(split) > 0:
        values = block_levels(rng, shape, split, -0.22, 0.18) * values
    return jnp.clip(values, min=-reach, max=reach).astype(kind)


def setup_inputs(seed: int = 0) -> dict:
    seeds = jax.random.split(jax.random.key(seed), 10)
    queries = draw_queries(jax.random.fold_in(seeds[9], 71), 0)
    keys = draw_keys(jax.random.fold_in(seeds[9], 71), 0)
    values = gaussian(seeds[2], (WINDOWS, WIN_LEN, D), 1.0, 6.0, ((0, 32), (1, 4)))
    resid = draw_resid(jax.random.fold_in(seeds[9], 71), 0)
    cotangent = gaussian(seeds[4], (WINDOWS, WIN_LEN, D), 0.05, 0.3125, ((0, 32), (1, 4)))
    zone_ids_keys = jax.random.split(jax.random.fold_in(seeds[5], 1), WINDOWS * WIN_LEN // SHARD_LEN)
    zone_ids_turns = jax.random.permutation(jax.random.fold_in(seeds[5], 3), WINDOWS * WIN_LEN // SHARD_LEN)
    zone_ids = jax.vmap(lambda own, number: routed_block(jax.random.fold_in(seeds[5], 2), own, number, SHARD_LEN, EXPERTS, 1, CAP, 2))(zone_ids_keys, zone_ids_turns).reshape((WINDOWS, WIN_LEN, 1))
    norm_gain = jnp.clip(1.0 + 0.18 * jax.random.normal(seeds[6], (D,), jnp.float32), 0.1, 1.9)
    w_in = gaussian(seeds[7], (EXPERTS, D, H), D ** -0.5, 0.125, ((0, 32), (2, 4)))
    w_out = gaussian(seeds[8], (EXPERTS, H, D), H ** -0.5, 0.09375, ((0, 32), (1, 4)))
    return {"queries": queries, "keys": keys, "values": values, "resid": resid, "cotangent": cotangent, "zone_ids": zone_ids, "norm_gain": norm_gain, "w_in": w_in, "w_out": w_out}


epsilon = 1e-05

def attend(query_win, key_win, value_win):
    length = query_win.shape[0]
    q_heads = query_win.astype(jnp.float32).reshape(length, HEADS, HEAD_DIM)
    k_heads = key_win.astype(jnp.float32).reshape(length, HEADS, HEAD_DIM)
    v_heads = value_win.astype(jnp.float32).reshape(length, HEADS, HEAD_DIM)
    scores = jnp.einsum('shd,thd->hst', q_heads, k_heads) * (1.0 / math.sqrt(HEAD_DIM))
    peak = lax.optimization_barrier(jnp.max(scores, axis=-1, keepdims=True))
    weights = jnp.exp(scores - peak)
    totals = lax.optimization_barrier(jnp.sum(weights, axis=-1))
    rounded = lax.optimization_barrier(weights.astype(jnp.bfloat16)).astype(jnp.float32)
    head_out = jnp.einsum('hst,thd->hsd', rounded, v_heads) / totals[..., None]
    return head_out.transpose(1, 0, 2).reshape(length, HEADS * HEAD_DIM)

def reference(queries, keys, values, resid, cotangent, zone_ids, norm_gain, w_in, w_out):
    attended = lax.map(lambda triple: attend(triple[0], triple[1], triple[2]), (queries, keys, values))
    mixed = resid.astype(jnp.float32) + attended
    mean_sq = lax.optimization_barrier(jnp.mean(mixed * mixed, axis=-1, keepdims=True))
    normed = (mixed * lax.rsqrt(mean_sq + epsilon) * norm_gain.astype(jnp.float32)).astype(jnp.bfloat16)
    flat_x = jnp.concatenate([normed.reshape(TOKENS, D), jnp.zeros((1, D), jnp.bfloat16)], 0)
    flat_g = jnp.concatenate([cotangent.reshape(TOKENS, D), jnp.zeros((1, D), jnp.bfloat16)], 0)
    zone_flat = zone_ids.reshape(TOKENS)

    def one_expert(expert):
        chosen = jnp.nonzero(zone_flat == expert, size=SLOTS, fill_value=TOKENS)[0]
        inputs = flat_x[chosen]
        grads_in = flat_g[chosen]
        pre_act = jnp.dot(inputs, w_in[expert], preferred_element_type=jnp.float32)
        activated, pull_back = jax.vjp(jax.nn.gelu, pre_act)
        hidden = activated.astype(jnp.bfloat16)
        expert_out = jnp.dot(hidden, w_out[expert], preferred_element_type=jnp.float32).astype(jnp.bfloat16)
        back_proj = jnp.dot(grads_in, w_out[expert].T, preferred_element_type=jnp.float32)
        d_pre = pull_back(back_proj)[0].astype(jnp.bfloat16)
        grad_first = jnp.dot(inputs.T, d_pre, preferred_element_type=jnp.float32).astype(jnp.bfloat16)
        grad_second = jnp.dot(hidden.T, grads_in, preferred_element_type=jnp.float32).astype(jnp.bfloat16)
        return (chosen, expert_out, grad_first, grad_second)
    chosen_all, outs_all, grad_w_in, grad_w_out = lax.map(one_expert, jnp.arange(EXPERTS, dtype=jnp.int32))
    summed = jnp.zeros((TOKENS + 1, D), jnp.float32).at[chosen_all.reshape(-1)].add(outs_all.reshape(-1, D).astype(jnp.float32))
    layer_out = (mixed.reshape(TOKENS, D) + summed[:TOKENS]).astype(jnp.bfloat16)
    return (layer_out.reshape(WINDOWS, WIN_LEN, D), grad_w_in, grad_w_out)
```

```python
import math

import jax
import jax.numpy as jnp
from jax import lax
from jax.experimental import pallas as pl
from jax.experimental.pallas import tpu as pltpu
from jax.sharding import PartitionSpec as P

HEADS = 16
CAPACITY = 10
EPS = 1e-05
F32 = jnp.float32
BF16 = jnp.bfloat16
MIB = 1 << 20


def params(mib, **kw):
    return pltpu.CompilerParams(vmem_limit_bytes=mib * MIB, **kw)


def cost(flops, nbytes, trans=0):
    return pl.CostEstimate(flops=flops, bytes_accessed=nbytes, transcendentals=trans)


def struct(shape, dtype=BF16):
    return jax.ShapeDtypeStruct(shape, dtype)


def dot(a, b, ca=1, cb=0):
    return lax.dot_general(a, b, (((ca,), (cb,)), ((), ())), preferred_element_type=F32)


def shift(x, axis, step):
    n = lax.axis_size(axis)
    return lax.ppermute(x, axis, [(i, (i + step) % n) for i in range(n)])


def split_kernel(me_ref, q_ref, k_ref, v_ref, *outs):
    width = outs[0].shape[2]
    for r, out in enumerate(outs):
        at = pl.multiple_of(((me_ref[0] + r) % 4) * width, width)
        for i, ref in enumerate((q_ref, k_ref, v_ref)):
            out[i] = ref[0, :, pl.ds(at, width)]


def split_heads(me, q, k, v):
    rows, width = q.shape[1], q.shape[2] // 4
    vm = pl.BlockSpec(memory_space=pltpu.VMEM)
    return pl.pallas_call(
        split_kernel,
        out_shape=[struct((3, rows, width))] * 4,
        in_specs=[pl.BlockSpec(memory_space=pltpu.SMEM), vm, vm, vm],
        out_specs=[vm] * 4,
        compiler_params=params(12),
        cost_estimate=cost(0, 3 << 20),
        name="split_heads",
    )(me, q, k, v)


def attention_kernel(scale, dim, p0, p1, p2, p3, o0, o1, o2, o3):
    pieces, outs = (p0, p1, p2, p3), (o0, o1, o2, o3)
    rows = p0.shape[1]
    for h in range(p0.shape[2] // dim):
        cols = slice(h * dim, (h + 1) * dim)
        k = jnp.concatenate([p[1, :, cols] for p in pieces], 0)
        v = jnp.concatenate([p[2, :, cols] for p in pieces], 0)
        q = jnp.concatenate([p[0, :, cols] for p in pieces], 0)
        scores = dot(q, k, 1, 1) * scale
        weights = jnp.exp(scores - jnp.max(scores, axis=-1, keepdims=True))
        totals = jnp.sum(weights, axis=-1, keepdims=True)
        res = dot(weights.astype(BF16), v) / totals
        for i, o in enumerate(outs):
            o[:, cols] = res[i * rows : (i + 1) * rows].astype(BF16)


def attention(pieces, dim):
    _, rows, width = pieces[0].shape
    vm = pl.BlockSpec(memory_space=pltpu.VMEM)
    scale = 1.0 / math.sqrt(dim)
    return pl.pallas_call(
        lambda *refs: attention_kernel(scale, dim, *refs),
        out_shape=[struct((rows, width))] * 4,
        in_specs=[vm] * 4,
        out_specs=[vm] * 4,
        compiler_params=params(28),
        cost_estimate=cost(16 * rows * rows * width * 4, 2 << 20, 1 << 20),
        name="attention",
    )(*pieces)


def place_rows(send_ref, tgt, parts):
    tokens = tgt.shape[1]
    chunk = 320
    for c in range(send_ref.shape[0] // chunk):
        row = lax.broadcasted_iota(jnp.int32, (chunk, tokens), 0) + c * chunk
        acc = None
        for q, part in enumerate(parts):
            hot = jnp.where(row == tgt + q * CAPACITY, 1.0, 0.0).astype(BF16)
            term = dot(hot, part)
            acc = term if acc is None else acc + term
        send_ref[c * chunk : (c + 1) * chunk, :] = acc.astype(BF16)


def route_kernel(owners, zone_ref, g_ref, tgt_ref, send_ref):
    zone = zone_ref[...]
    tokens = zone.shape[1]
    hot = jnp.where(lax.broadcasted_iota(jnp.int32, (owners, tokens), 0) == zone, 1.0, 0.0)
    upper = jnp.where(
        lax.broadcasted_iota(jnp.int32, (tokens, tokens), 0)
        <= lax.broadcasted_iota(jnp.int32, (tokens, tokens), 1),
        1.0,
        0.0,
    )
    rank = dot(hot.astype(BF16), upper.astype(BF16))
    slot = jnp.sum(hot * rank, axis=0, keepdims=True) - 1.0
    tgt = zone * (4 * CAPACITY) + slot.astype(jnp.int32)
    tgt_ref[...] = tgt
    width = send_ref.shape[1]
    place_rows(send_ref, tgt, [g_ref[0, :, q * width : (q + 1) * width] for q in range(4)])


def route(zone_row, cot, owners):
    tokens, model = cot.shape[1], cot.shape[2]
    vm = pl.BlockSpec(memory_space=pltpu.VMEM)
    return pl.pallas_call(
        lambda *refs: route_kernel(owners, *refs),
        out_shape=[struct((1, tokens), jnp.int32), struct((owners * 4 * CAPACITY, model // 4))],
        in_specs=[vm] * 2,
        out_specs=[vm] * 2,
        compiler_params=params(16),
        cost_estimate=cost(700_000_000, 2 << 20),
        name="route",
    )(zone_row, cot)


def norm_kernel(me_ref, a0, a1, a2, a3, resid_ref, gain_ref, tgt_ref, mixed_ref, send_ref):
    width = a0.shape[1]
    for r, a in enumerate((a0, a1, a2, a3)):
        cols = pl.ds(pl.multiple_of(((me_ref[0] + r) % 4) * width, width), width)
        mixed_ref[:, cols] = resid_ref[0, :, cols].astype(F32) + a[...].astype(F32)
    mixed = mixed_ref[...]
    inv = lax.rsqrt(jnp.mean(mixed * mixed, axis=-1, keepdims=True) + EPS)
    normed = (mixed * inv * gain_ref[...]).astype(BF16)
    place_rows(send_ref, tgt_ref[...], [normed[:, q * width : (q + 1) * width] for q in range(4)])


def norm(me, att, resid, gain, tgt, owners):
    tokens, model = resid.shape[1], resid.shape[2]
    vm = pl.BlockSpec(memory_space=pltpu.VMEM)
    return pl.pallas_call(
        norm_kernel,
        out_shape=[struct((tokens, model), F32), struct((owners * 4 * CAPACITY, model // 4))],
        in_specs=[pl.BlockSpec(memory_space=pltpu.SMEM)] + [vm] * 7,
        out_specs=[vm] * 2,
        compiler_params=params(20),
        cost_estimate=cost(700_000_000, 4 << 20),
        name="norm",
    )(me, *att, resid, gain, tgt)


def regroup(size):
    per = size // 4
    row = lax.broadcasted_iota(jnp.int32, (size, size), 0)
    col = lax.broadcasted_iota(jnp.int32, (size, size), 1)
    quarter, rest = row // per, row % per
    want = (rest // CAPACITY) * (4 * CAPACITY) + quarter * CAPACITY + rest % CAPACITY
    return jnp.where(col == want, 1.0, 0.0).astype(BF16)


def unpack_kernel(hot_ref, got_ref, *outs):
    size = hot_ref.shape[0]
    per, width = size // 4, got_ref.shape[1]
    groups = got_ref.shape[0] // size
    each = groups // len(outs)
    for g in range(groups):
        rows = dot(hot_ref[...], got_ref[g * size : (g + 1) * size, :]).astype(BF16)
        at = (g % each) * per
        for q in range(4):
            outs[g // each][at : at + per, q * width : (q + 1) * width] = rows[
                q * per : (q + 1) * per
            ]


def unpack(hot, got, halves):
    rows, width = got.shape
    vm = pl.BlockSpec(memory_space=pltpu.VMEM)
    return pl.pallas_call(
        unpack_kernel,
        out_shape=[struct((rows // 4 // halves, width * 4))] * halves,
        in_specs=[vm] * 2,
        out_specs=[vm] * halves,
        compiler_params=params(14),
        cost_estimate=cost(420_000_000, 3 << 20),
        name="unpack",
    )(hot, got)


def pack_kernel(hot_ref, oa, ob, fa, fb, ga, gb, send_ref):
    size = hot_ref.shape[0]
    per, width = size // 4, send_ref.shape[1]
    groups = send_ref.shape[0] // size
    each = groups // 2
    for g in range(groups):
        trio = (oa, fa, ga) if g < each else (ob, fb, gb)
        at = slice((g % each) * per, (g % each) * per + per)
        total = sum(t[at, :].astype(F32) for t in trio[1:]) + trio[0][at, :].astype(F32)
        total = total.astype(BF16)
        stack = jnp.concatenate([total[:, q * width : (q + 1) * width] for q in range(4)], 0)
        send_ref[g * size : (g + 1) * size, :] = dot(hot_ref[...], stack, 0, 0).astype(BF16)


def pack(hot, six):
    rows, model = six[0].shape
    vm = pl.BlockSpec(memory_space=pltpu.VMEM)
    return pl.pallas_call(
        pack_kernel,
        out_shape=struct((rows * 8, model // 4)),
        in_specs=[vm] * 7,
        out_specs=vm,
        compiler_params=params(20),
        cost_estimate=cost(420_000_000, 6 << 20),
        name="pack",
    )(hot, *six)


def final_kernel(tgt_ref, mixed_ref, got_ref, out_ref):
    tgt = tgt_ref[...]
    tokens, width = tgt.shape[1], got_ref.shape[1]
    row = lax.broadcasted_iota(jnp.int32, (got_ref.shape[0], tokens), 0)
    got = got_ref[...]
    for q in range(4):
        hot = jnp.where(row == tgt + q * CAPACITY, 1.0, 0.0).astype(BF16)
        cols = slice(q * width, (q + 1) * width)
        out_ref[0, :, cols] = (mixed_ref[:, cols] + dot(hot, got, 0, 0)).astype(BF16)


def final(tgt, mixed, got):
    vm = pl.BlockSpec(memory_space=pltpu.VMEM)
    return pl.pallas_call(
        final_kernel,
        out_shape=struct((1,) + mixed.shape),
        in_specs=[vm] * 3,
        out_specs=vm,
        compiler_params=params(16),
        cost_estimate=cost(700_000_000, 3 << 20),
        name="combine",
    )(tgt, mixed, got)


def expert_kernel(plane_ref, xa, xb, g_ref, win, wout, hid_ref, dpre_ref, oa, ob, x_all, acc):
    step = pl.program_id(0)
    half = xa.shape[0]

    @pl.when(step == 0)
    def _():
        x_all[:half] = xa[...]
        x_all[half:] = xb[...]

    pre = dot(x_all[...], win[0])
    act, pull = jax.vjp(jax.nn.gelu, pre)
    hidden = act.astype(BF16)
    hid_ref[...] = hidden
    back = dot(g_ref[...], wout[0], 1, 1)
    dpre_ref[...] = pull(back)[0].astype(BF16)
    term = dot(hidden, wout[0])

    @pl.when(step == 0)
    def _():
        acc[...] = term

    @pl.when(step > 0)
    def _():
        acc[...] += term

    @pl.when(step == pl.num_programs(0) - 1)
    def _():
        oa[...] = acc[:half].astype(BF16)
        ob[...] = acc[half:].astype(BF16)


def expert(plane, xa, xb, g_all, w_in, w_out):
    half, model = xa.shape
    rows, hidden = 2 * half, w_in.shape[2]
    block = 256
    whole = pl.BlockSpec((half, model), lambda j, p: (0, 0))
    part = pl.BlockSpec((rows, block), lambda j, p: (0, j))
    return pl.pallas_call(
        expert_kernel,
        grid_spec=pltpu.PrefetchScalarGridSpec(
            num_scalar_prefetch=1,
            grid=(hidden // block,),
            in_specs=[
                whole,
                whole,
                pl.BlockSpec((rows, model), lambda j, p: (p[0], 0)),
                pl.BlockSpec((1, model, block), lambda j, p: (0, 0, j)),
                pl.BlockSpec((1, block, model), lambda j, p: (0, j, 0)),
            ],
            out_specs=[part, part, whole, whole],
            scratch_shapes=[pltpu.VMEM((rows, model), BF16), pltpu.VMEM((rows, model), F32)],
        ),
        out_shape=[struct((rows, hidden))] * 2 + [struct((half, model))] * 2,
        compiler_params=params(32),
        cost_estimate=cost(6 * rows * model * hidden, 12 << 20, rows * hidden),
        name="expert",
    )(plane, xa, xb, g_all, w_in, w_out)


def grad_kernel(planes, *refs):
    xs, ds, hs, gs = refs[:8], refs[8:12], refs[12:16], refs[16:20]
    first, second, x_all, d_all, h_all, g_all = refs[20:]
    step = pl.program_id(0)
    rows = ds[0].shape[0]

    @pl.when(step == 0)
    def _():
        for i in range(4):
            d_all[i * rows : (i + 1) * rows] = ds[i][...]
            g_all[i * rows : (i + 1) * rows] = gs[i][...]

    half = rows // 2
    for i in range(8):
        x_all[i * half : (i + 1) * half] = xs[i][...]
    for i in range(4):
        h_all[i * rows : (i + 1) * rows] = hs[i][...]
    first[0] = dot(x_all[...], d_all[...], 0, 0).astype(BF16)
    second[0] = dot(h_all[...], g_all[...], 0, 0).astype(BF16)


def grads(planes, xs, ds, hs, g_all):
    half, model = xs[0].shape
    rows, hidden = ds[0].shape
    steps = 8
    xb, hb = model // steps, hidden // steps
    whole = lambda r, c: pl.BlockSpec((r, c), lambda j, p: (0, 0))

    def g_spec(i):
        return pl.BlockSpec((rows, model), lambda j, p: (p[i], 0))

    return pl.pallas_call(
        grad_kernel,
        grid_spec=pltpu.PrefetchScalarGridSpec(
            num_scalar_prefetch=1,
            grid=(steps,),
            in_specs=[pl.BlockSpec((half, xb), lambda j, p: (0, j))] * 8
            + [whole(rows, hidden)] * 4
            + [pl.BlockSpec((rows, hb), lambda j, p: (0, j))] * 4
            + [g_spec(i) for i in range(4)],
            out_specs=[
                pl.BlockSpec((1, xb, hidden), lambda j, p: (0, j, 0)),
                pl.BlockSpec((1, hb, model), lambda j, p: (0, j, 0)),
            ],
            scratch_shapes=[
                pltpu.VMEM((4 * rows, xb), BF16),
                pltpu.VMEM((4 * rows, hidden), BF16),
                pltpu.VMEM((4 * rows, hb), BF16),
                pltpu.VMEM((4 * rows, model), BF16),
            ],
        ),
        out_shape=[struct((1, model, hidden)), struct((1, hidden, model))],
        compiler_params=params(44),
        cost_estimate=cost(16 * rows * model * hidden, 24 << 20),
        name="grads",
    )(planes, *xs, *ds, *hs, *([g_all] * 4))


def shards(queries, keys, values, resid, cotangent, zone_ids, norm_gain, w_in, w_out):
    model = queries.shape[2]
    owners = lax.axis_size("seq") * lax.axis_size("expert")
    seq_at = lax.axis_index("seq").astype(jnp.int32).reshape(1)
    dp_at = lax.axis_index("dp").astype(jnp.int32)
    planes = [((dp_at + r) % 4).reshape(1) for r in (0, 3, 1, 2)]

    def exchange(blocks):
        shaped = blocks.reshape(owners, 4 * CAPACITY, model // 4)
        got = lax.all_to_all(shaped, ("seq", "expert"), 0, 0, tiled=True)
        return got.reshape(owners * 4 * CAPACITY, model // 4)

    hot = regroup(8 * 4 * CAPACITY)
    sent = split_heads(seq_at, queries, keys, values)
    pieces = [sent[0]] + [shift(sent[r], "seq", r) for r in (1, 2, 3)]
    tgt, send_g = route(zone_ids[:, :, 0], cotangent, owners)
    (own_g,) = unpack(hot, exchange(send_g), 1)
    g_all = lax.all_gather(own_g, "dp", axis=0, tiled=True)

    att = attention(pieces, model // HEADS)
    att = [att[0]] + [shift(att[r], "seq", -r) for r in (1, 2, 3)]
    mixed, send_x = norm(seq_at, att, resid, norm_gain.reshape(1, model), tgt, owners)
    oxa, oxb = unpack(hot, exchange(send_x), 2)
    fxa, gxb = shift(oxa, "dp", 1), shift(oxb, "dp", -1)
    fxb, gxa = shift(oxb, "dp", 1), shift(oxa, "dp", -1)
    hxa, hxb = shift(fxa, "dp", 1), shift(gxb, "dp", -1)

    pairs = [(oxa, oxb), (fxa, fxb), (gxa, gxb), (hxa, hxb)]
    done = [expert(p, a, b, g_all, w_in, w_out) for p, (a, b) in zip(planes, pairs)]
    (own_a, own_b), (prev_a, prev_b), (next_a, next_b), (far_a, far_b) = [d[2:] for d in done]
    to_next_b = shift(next_b, "dp", 1)
    to_prev_a = shift(prev_a, "dp", -1)
    via_a = shift(far_a, "dp", 1)
    via_b = shift(far_b, "dp", -1)
    next_a = (next_a.astype(F32) + via_a.astype(F32)).astype(BF16)
    prev_b = (prev_b.astype(F32) + via_b.astype(F32)).astype(BF16)
    to_next_a = shift(next_a, "dp", 1)
    to_prev_b = shift(prev_b, "dp", -1)
    grad_first, grad_second = grads(
        jnp.concatenate(planes),
        [x for pair in pairs for x in pair],
        [d[1] for d in done],
        [d[0] for d in done],
        g_all,
    )
    back = pack(hot, [own_a, own_b, to_next_a, to_next_b, to_prev_a, to_prev_b])
    layer_out = final(tgt, mixed, exchange(back))
    return (layer_out, grad_first, grad_second)


def solution(mesh):
    token = P(("dp", "expert"), "seq", None)
    first = P(("seq", "expert"), None, "dp")
    second = P(("seq", "expert"), "dp", None)
    return jax.shard_map(
        shards,
        mesh=mesh,
        in_specs=(token,) * 6 + (P(), first, second),
        out_specs=(token, first, second),
        check_vma=False,
    )
```

```python
import math

import jax
import jax.numpy as jnp
from jax import lax
from jax.experimental import pallas as pl
from jax.experimental.pallas import tpu as pltpu
from jax.sharding import PartitionSpec as P

HEADS = 16
CAPACITY = 10
EPS = 1e-05
F32 = jnp.float32
BF16 = jnp.bfloat16
MIB = 1 << 20


def params(mib, **kw):
    return pltpu.CompilerParams(vmem_limit_bytes=mib * MIB, **kw)


def cost(flops, nbytes, trans=0):
    return pl.CostEstimate(flops=flops, bytes_accessed=nbytes, transcendentals=trans)


def struct(shape, dtype=BF16):
    return jax.ShapeDtypeStruct(shape, dtype)


def dot(a, b, ca=1, cb=0):
    return lax.dot_general(a, b, (((ca,), (cb,)), ((), ())), preferred_element_type=F32)


def shift(x, axis, step):
    n = lax.axis_size(axis)
    return lax.ppermute(x, axis, [(i, (i + step) % n) for i in range(n)])


def split_kernel(me_ref, q_ref, k_ref, v_ref, *outs):
    width = outs[0].shape[2]
    for r, out in enumerate(outs):
        at = pl.multiple_of(((me_ref[0] + r) % 4) * width, width)
        for i, ref in enumerate((q_ref, k_ref, v_ref)):
            out[i] = ref[0, :, pl.ds(at, width)]


def split_heads(me, q, k, v):
    rows, width = q.shape[1], q.shape[2] // 4
    vm = pl.BlockSpec(memory_space=pltpu.VMEM)
    return pl.pallas_call(
        split_kernel,
        out_shape=[struct((3, rows, width))] * 4,
        in_specs=[pl.BlockSpec(memory_space=pltpu.SMEM), vm, vm, vm],
        out_specs=[vm] * 4,
        compiler_params=params(12),
        cost_estimate=cost(0, 3 << 20),
        name="split_heads",
    )(me, q, k, v)


def attention_kernel(scale, dim, p0, p1, p2, p3, o0, o1, o2, o3):
    pieces, outs = (p0, p1, p2, p3), (o0, o1, o2, o3)
    rows = p0.shape[1]
    for h in range(p0.shape[2] // dim):
        cols = slice(h * dim, (h + 1) * dim)
        k = jnp.concatenate([p[1, :, cols] for p in pieces], 0)
        v = jnp.concatenate([p[2, :, cols] for p in pieces], 0)
        q = jnp.concatenate([p[0, :, cols] for p in pieces], 0)
        scores = dot(q, k, 1, 1) * scale
        weights = jnp.exp(scores - jnp.max(scores, axis=-1, keepdims=True))
        totals = jnp.sum(weights, axis=-1, keepdims=True)
        res = dot(weights.astype(BF16), v) / totals
        for i, o in enumerate(outs):
            o[:, cols] = res[i * rows : (i + 1) * rows].astype(BF16)


def attention(pieces, dim):
    _, rows, width = pieces[0].shape
    vm = pl.BlockSpec(memory_space=pltpu.VMEM)
    scale = 1.0 / math.sqrt(dim)
    return pl.pallas_call(
        lambda *refs: attention_kernel(scale, dim, *refs),
        out_shape=[struct((rows, width))] * 4,
        in_specs=[vm] * 4,
        out_specs=[vm] * 4,
        compiler_params=params(28),
        cost_estimate=cost(16 * rows * rows * width * 4, 2 << 20, 1 << 20),
        name="attention",
    )(*pieces)


def place_rows(send_ref, tgt, parts):
    tokens = tgt.shape[1]
    chunk = send_ref.shape[0] // 4
    for c in range(4):
        row = lax.broadcasted_iota(jnp.int32, (chunk, tokens), 0) + c * chunk
        acc = None
        for q, part in enumerate(parts):
            hot = jnp.where(row == tgt + q * CAPACITY, 1.0, 0.0).astype(BF16)
            term = dot(hot, part)
            acc = term if acc is None else acc + term
        send_ref[c * chunk : (c + 1) * chunk, :] = acc.astype(BF16)


def route_kernel(owners, zone_ref, g_ref, tgt_ref, send_ref):
    zone = zone_ref[...]
    tokens = zone.shape[1]
    hot = jnp.where(lax.broadcasted_iota(jnp.int32, (owners, tokens), 0) == zone, 1.0, 0.0)
    upper = jnp.where(
        lax.broadcasted_iota(jnp.int32, (tokens, tokens), 0)
        <= lax.broadcasted_iota(jnp.int32, (tokens, tokens), 1),
        1.0,
        0.0,
    )
    rank = dot(hot.astype(BF16), upper.astype(BF16))
    slot = jnp.sum(hot * rank, axis=0, keepdims=True) - 1.0
    tgt = zone * (4 * CAPACITY) + slot.astype(jnp.int32)
    tgt_ref[...] = tgt
    width = send_ref.shape[1]
    place_rows(send_ref, tgt, [g_ref[0, :, q * width : (q + 1) * width] for q in range(4)])


def route(zone_row, cot, owners):
    tokens, model = cot.shape[1], cot.shape[2]
    vm = pl.BlockSpec(memory_space=pltpu.VMEM)
    return pl.pallas_call(
        lambda *refs: route_kernel(owners, *refs),
        out_shape=[struct((1, tokens), jnp.int32), struct((owners * 4 * CAPACITY, model // 4))],
        in_specs=[vm] * 2,
        out_specs=[vm] * 2,
        compiler_params=params(16),
        cost_estimate=cost(700_000_000, 2 << 20),
        name="route",
    )(zone_row, cot)


def norm_kernel(me_ref, a0, a1, a2, a3, resid_ref, gain_ref, tgt_ref, mixed_ref, *sends):
    width = a0.shape[1]
    for r, a in enumerate((a0, a1, a2, a3)):
        cols = pl.ds(pl.multiple_of(((me_ref[0] + r) % 4) * width, width), width)
        mixed_ref[:, cols] = resid_ref[0, :, cols].astype(F32) + a[...].astype(F32)
    mixed = mixed_ref[...]
    inv = lax.rsqrt(jnp.mean(mixed * mixed, axis=-1, keepdims=True) + EPS)
    normed = (mixed * inv * gain_ref[...]).astype(BF16)
    part = sends[0].shape[1]
    for i, send in enumerate(sends):
        parts = [normed[:, (i * 4 + q) * part : (i * 4 + q + 1) * part] for q in range(4)]
        place_rows(send, tgt_ref[...], parts)


def norm(me, att, resid, gain, tgt, owners):
    tokens, model = resid.shape[1], resid.shape[2]
    vm = pl.BlockSpec(memory_space=pltpu.VMEM)
    return pl.pallas_call(
        norm_kernel,
        out_shape=[struct((tokens, model), F32)]
        + [struct((owners * 4 * CAPACITY, model // 8))] * 2,
        in_specs=[pl.BlockSpec(memory_space=pltpu.SMEM)] + [vm] * 7,
        out_specs=[vm] * 3,
        compiler_params=params(20),
        cost_estimate=cost(700_000_000, 4 << 20),
        name="norm",
    )(me, *att, resid, gain, tgt)


def regroup(size):
    per = size // 4
    row = lax.broadcasted_iota(jnp.int32, (size, size), 0)
    col = lax.broadcasted_iota(jnp.int32, (size, size), 1)
    quarter, rest = row // per, row % per
    want = (rest // CAPACITY) * (4 * CAPACITY) + quarter * CAPACITY + rest % CAPACITY
    return jnp.where(col == want, 1.0, 0.0).astype(BF16)


def unpack_kernel(hot_ref, got_ref, out):
    size = hot_ref.shape[0]
    per, width = size // 4, got_ref.shape[1]
    for g in range(got_ref.shape[0] // size):
        rows = dot(hot_ref[...], got_ref[g * size : (g + 1) * size, :]).astype(BF16)
        for q in range(4):
            out[g * per : (g + 1) * per, q * width : (q + 1) * width] = rows[
                q * per : (q + 1) * per
            ]


def unpack(hot, got):
    rows, width = got.shape
    vm = pl.BlockSpec(memory_space=pltpu.VMEM)
    return pl.pallas_call(
        unpack_kernel,
        out_shape=struct((rows // 4, width * 4)),
        in_specs=[vm] * 2,
        out_specs=vm,
        compiler_params=params(14),
        cost_estimate=cost(1000, 1 << 10),
        name="unpack",
    )(hot, got)


def pack_kernel(hot_ref, o0, o1, f0, f1, g0, g1, send_ref):
    size = hot_ref.shape[0]
    per, width = size // 4, send_ref.shape[1]
    for g in range(send_ref.shape[0] // size):
        at = slice(g * per, (g + 1) * per)
        stack = []
        for own, prev, after in ((o0, f0, g0), (o1, f1, g1)):
            total = own[at, :].astype(F32) + prev[at, :].astype(F32) + after[at, :].astype(F32)
            total = total.astype(BF16)
            stack += [total[:, :width], total[:, width:]]
        send_ref[g * size : (g + 1) * size, :] = dot(
            hot_ref[...], jnp.concatenate(stack, 0), 0, 0
        ).astype(BF16)


def pack(hot, sums):
    rows, width = sums[0].shape
    vm = pl.BlockSpec(memory_space=pltpu.VMEM)
    return pl.pallas_call(
        pack_kernel,
        out_shape=struct((rows * 4, width // 2)),
        in_specs=[vm] * 7,
        out_specs=vm,
        compiler_params=params(20),
        cost_estimate=cost(420_000_000, 6 << 20),
        name="pack",
    )(hot, *sums)


def final_kernel(tgt_ref, mixed_ref, got_ref, out_ref):
    tgt = tgt_ref[...]
    tokens, width = tgt.shape[1], got_ref.shape[1]
    row = lax.broadcasted_iota(jnp.int32, (got_ref.shape[0], tokens), 0)
    got = got_ref[...]
    for q in range(4):
        hot = jnp.where(row == tgt + q * CAPACITY, 1.0, 0.0).astype(BF16)
        cols = slice(q * width, (q + 1) * width)
        out_ref[0, :, cols] = (mixed_ref[:, cols] + dot(hot, got, 0, 0)).astype(BF16)


def final(tgt, mixed, got):
    vm = pl.BlockSpec(memory_space=pltpu.VMEM)
    return pl.pallas_call(
        final_kernel,
        out_shape=struct((1,) + mixed.shape),
        in_specs=[vm] * 3,
        out_specs=vm,
        compiler_params=params(16),
        cost_estimate=cost(700_000_000, 3 << 20),
        name="combine",
    )(tgt, mixed, got)


def forward(x0, x1, w_in, w_out):
    width = x0.shape[1]
    pre = dot(x0, w_in[:width]) + dot(x1, w_in[width:])
    hidden = jax.nn.gelu(pre).astype(BF16)
    return pre, hidden, dot(hidden, w_out).astype(BF16)


def backward(pre, back):
    pull = jax.vjp(jax.nn.gelu, pre)[1]
    return pull(back)[0].astype(BF16)


def expert_part(planes, ours, prevs, nexts, g_all, back, w_in, w_out):
    x0, x1 = ours
    rows, width = x0.shape
    own_pre, own_h, own = forward(x0, x1, w_in, w_out)
    *prevs, n0, n1, own, own_h, own_pre = lax.optimization_barrier(
        (*prevs, *nexts, own, own_h, own_pre)
    )
    p0, p1 = prevs
    far0, far1 = shift(p0, "dp", 1), shift(n1, "dp", -1)
    prev_pre, prev_h, prev = forward(p0, p1, w_in, w_out)
    next_pre, next_h, after = forward(n0, n1, w_in, w_out)
    to_prev0 = shift(prev[:, :width], "dp", -1)
    to_next1 = shift(after[:, width:], "dp", 1)
    far0, far1, prev, after, prev_pre, next_pre, prev_h, next_h = lax.optimization_barrier(
        (far0, far1, prev, after, prev_pre, next_pre, prev_h, next_h)
    )
    far_pre, far_h, far = forward(far0, far1, w_in, w_out)
    via0, via1 = shift(far[:, :width], "dp", 1), shift(far[:, width:], "dp", -1)
    back, far_pre, far_h, _ = lax.optimization_barrier((back, far_pre, far_h, far))
    d_rows = jnp.concatenate(
        [
            backward(pre, lax.dynamic_slice(back, (planes[r] * rows, 0), pre.shape))
            for r, pre in ((0, own_pre), (3, prev_pre), (1, next_pre), (2, far_pre))
        ],
        0,
    )
    x_rows = jnp.concatenate(
        [
            jnp.concatenate([x0, p0, n0, far0], 0),
            jnp.concatenate([x1, p1, n1, far1], 0),
        ],
        1,
    )
    h_rows = jnp.zeros((4 * rows, w_in.shape[1]), BF16)
    for r, h in ((0, own_h), (3, prev_h), (1, next_h), (2, far_h)):
        h_rows = lax.dynamic_update_slice(h_rows, h, (planes[r] * rows, 0))
    grad_second = dot(h_rows, g_all, 0, 0).astype(BF16)
    via0, via1, grad_second = lax.optimization_barrier((via0, via1, grad_second))
    sum0 = (after[:, :width].astype(F32) + via0.astype(F32)).astype(BF16)
    sum1 = (prev[:, width:].astype(F32) + via1.astype(F32)).astype(BF16)
    to_next0, to_prev1 = shift(sum0, "dp", 1), shift(sum1, "dp", -1)
    grad_first = dot(x_rows, d_rows, 0, 0).astype(BF16)
    sums = [own[:, :width], own[:, width:], to_next0, to_next1, to_prev0, to_prev1]
    return sums, grad_first, grad_second


def shards(queries, keys, values, resid, cotangent, zone_ids, norm_gain, w_in, w_out):
    model = queries.shape[2]
    owners = lax.axis_size("seq") * lax.axis_size("expert")
    seq_at = lax.axis_index("seq").astype(jnp.int32).reshape(1)
    dp_at = lax.axis_index("dp").astype(jnp.int32)
    planes = jnp.stack([(dp_at + r) % 4 for r in range(4)])

    def exchange(blocks):
        shaped = blocks.reshape(owners, 4 * CAPACITY, -1)
        return lax.all_to_all(shaped, ("seq", "expert"), 0, 0, tiled=True)

    def flat(blocks):
        return blocks.reshape(-1, blocks.shape[-1])

    hot = regroup(8 * 4 * CAPACITY)
    tgt, send_g = route(zone_ids[:, :, 0], cotangent, owners)
    own_g = unpack(hot, flat(exchange(send_g)))
    g_all = lax.all_gather(own_g, "dp", axis=0, tiled=True)

    sent = split_heads(seq_at, queries, keys, values)
    pieces = [sent[0]] + [shift(sent[r], "seq", r) for r in (1, 2, 3)]
    att = attention(pieces, model // HEADS)
    *att, _ = lax.optimization_barrier((*att, own_g))
    att = [att[0]] + [shift(att[r], "seq", -r) for r in (1, 2, 3)]
    mixed, send0, send1 = norm(seq_at, att, resid, norm_gain.reshape(1, model), tgt, owners)
    x0 = unpack(hot, flat(exchange(send0)))
    p0, n0 = shift(x0, "dp", 1), shift(x0, "dp", -1)
    send1, _ = lax.optimization_barrier((send1, x0))
    back = dot(g_all, w_out[0], 1, 1)
    got1, back = lax.optimization_barrier((exchange(send1), back))
    x1 = unpack(hot, flat(got1))
    p1, n1 = shift(x1, "dp", 1), shift(x1, "dp", -1)
    sums, grad_first, grad_second = expert_part(
        planes, (x0, x1), (p0, p1), (n0, n1), g_all, back, w_in[0], w_out[0]
    )
    packed = pack(hot, sums)
    layer_out = final(tgt, mixed, flat(exchange(packed)))
    return (layer_out, grad_first[None], grad_second[None])


def solution(mesh):
    token = P(("dp", "expert"), "seq", None)
    first = P(("seq", "expert"), None, "dp")
    second = P(("seq", "expert"), "dp", None)
    return jax.shard_map(
        shards,
        mesh=mesh,
        in_specs=(token,) * 6 + (P(), first, second),
        out_specs=(token, first, second),
        check_vma=False,
    )
```

```python
import math

import jax
import jax.numpy as jnp
from jax import lax
from jax.experimental import pallas as pl
from jax.experimental.pallas import tpu as pltpu
from jax.sharding import PartitionSpec as P

HEADS = 16
CAPACITY = 10
EPS = 1e-05
F32 = jnp.float32
BF16 = jnp.bfloat16
MIB = 1 << 20


def params(mib, **kw):
    return pltpu.CompilerParams(vmem_limit_bytes=mib * MIB, **kw)


def cost(flops, nbytes, trans=0):
    return pl.CostEstimate(flops=flops, bytes_accessed=nbytes, transcendentals=trans)


def struct(shape, dtype=BF16):
    return jax.ShapeDtypeStruct(shape, dtype)


def dot(a, b, ca=1, cb=0):
    return lax.dot_general(a, b, (((ca,), (cb,)), ((), ())), preferred_element_type=F32)


def shift(x, axis, step):
    n = lax.axis_size(axis)
    return lax.ppermute(x, axis, [(i, (i + step) % n) for i in range(n)])


def split_kernel(me_ref, q_ref, k_ref, v_ref, *outs):
    width = outs[0].shape[2]
    for r, out in enumerate(outs):
        at = pl.multiple_of(((me_ref[0] + r) % 4) * width, width)
        for i, ref in enumerate((q_ref, k_ref, v_ref)):
            out[i] = ref[0, :, pl.ds(at, width)]


def split_heads(me, q, k, v):
    rows, width = q.shape[1], q.shape[2] // 4
    vm = pl.BlockSpec(memory_space=pltpu.VMEM)
    return pl.pallas_call(
        split_kernel,
        out_shape=[struct((3, rows, width))] * 4,
        in_specs=[pl.BlockSpec(memory_space=pltpu.SMEM), vm, vm, vm],
        out_specs=[vm] * 4,
        compiler_params=params(12),
        cost_estimate=cost(0, 3 << 20),
        name="split_heads",
    )(me, q, k, v)


def attention_kernel(scale, dim, p0, p1, p2, p3, o0, o1, o2, o3):
    pieces, outs = (p0, p1, p2, p3), (o0, o1, o2, o3)
    rows = p0.shape[1]
    for h in range(p0.shape[2] // dim):
        cols = slice(h * dim, (h + 1) * dim)
        k = jnp.concatenate([p[1, :, cols] for p in pieces], 0)
        v = jnp.concatenate([p[2, :, cols] for p in pieces], 0)
        q = jnp.concatenate([p[0, :, cols] for p in pieces], 0)
        scores = dot(q, k, 1, 1) * scale
        weights = jnp.exp(scores - jnp.max(scores, axis=-1, keepdims=True))
        totals = jnp.sum(weights, axis=-1, keepdims=True)
        res = dot(weights.astype(BF16), v) / totals
        for i, o in enumerate(outs):
            o[:, cols] = res[i * rows : (i + 1) * rows].astype(BF16)


def attention(pieces, dim):
    _, rows, width = pieces[0].shape
    vm = pl.BlockSpec(memory_space=pltpu.VMEM)
    scale = 1.0 / math.sqrt(dim)
    return pl.pallas_call(
        lambda *refs: attention_kernel(scale, dim, *refs),
        out_shape=[struct((rows, width))] * 4,
        in_specs=[vm] * 4,
        out_specs=[vm] * 4,
        compiler_params=params(28),
        cost_estimate=cost(16 * rows * rows * width * 4, 2 << 20, 1 << 20),
        name="attention",
    )(*pieces)


def place_rows(send_ref, tgt, parts):
    tokens = tgt.shape[1]
    chunk = send_ref.shape[0] // 4
    for c in range(4):
        row = lax.broadcasted_iota(jnp.int32, (chunk, tokens), 0) + c * chunk
        acc = None
        for q, part in enumerate(parts):
            hot = jnp.where(row == tgt + q * CAPACITY, 1.0, 0.0).astype(BF16)
            term = dot(hot, part)
            acc = term if acc is None else acc + term
        send_ref[c * chunk : (c + 1) * chunk, :] = acc.astype(BF16)


def slots_of(zone, owners):
    tokens = zone.shape[1]
    hot = jnp.where(lax.broadcasted_iota(jnp.int32, (owners, tokens), 0) == zone, 1.0, 0.0)
    upper = jnp.where(
        lax.broadcasted_iota(jnp.int32, (tokens, tokens), 0)
        <= lax.broadcasted_iota(jnp.int32, (tokens, tokens), 1),
        1.0,
        0.0,
    )
    rank = dot(hot.astype(BF16), upper.astype(BF16))
    slot = jnp.sum(hot * rank, axis=0, keepdims=True) - 1.0
    return zone * (4 * CAPACITY) + slot.astype(jnp.int32)


def slots(zone_row, owners):
    def kernel(zone_ref, tgt_ref):
        tgt_ref[...] = slots_of(zone_ref[...], owners)

    vm = pl.BlockSpec(memory_space=pltpu.VMEM)
    return pl.pallas_call(
        kernel,
        out_shape=struct(zone_row.shape, jnp.int32),
        in_specs=[vm],
        out_specs=vm,
        compiler_params=params(4),
        cost_estimate=cost(1_000_000, 1000),
        name="slots",
    )(zone_row)


def route_kernel(owners, order_ref, zone_ref, g_ref, send_ref):
    width = send_ref.shape[2]
    block = 4 * CAPACITY
    rows = 8 * block
    for pair in range(2):
        tgts = [slots_of(zone_ref[pair * 2 + j], owners) for j in range(2)]
        for c in range(owners // 8):
            got = []
            for j in range(2):
                row = lax.broadcasted_iota(jnp.int32, (rows, tgts[j].shape[1]), 0) + c * rows
                acc = None
                for q in range(4):
                    hot = jnp.where(row == tgts[j] + q * CAPACITY, 1.0, 0.0).astype(BF16)
                    plane = order_ref[pair * 2 + j]
                    term = dot(hot, g_ref[plane, :, q * width : (q + 1) * width])
                    acc = term if acc is None else acc + term
                got.append(acc.reshape(8, block, width))
            both = jnp.concatenate(got, 1).astype(BF16)
            send_ref[c * 8 : (c + 1) * 8, pair * 2 * block : (pair + 1) * 2 * block, :] = both


def route(order, zones, g_planes, owners):
    model = g_planes.shape[2]
    vm = pl.BlockSpec(memory_space=pltpu.VMEM)
    return pl.pallas_call(
        lambda *refs: route_kernel(owners, *refs),
        out_shape=struct((owners, 16 * CAPACITY, model // 4)),
        in_specs=[pl.BlockSpec(memory_space=pltpu.SMEM), vm, vm],
        out_specs=vm,
        compiler_params=params(32),
        cost_estimate=cost(2_700_000_000, 8 << 20),
        name="route",
    )(order, zones, g_planes)


def unroute_kernel(hot_ref, got_ref, out_ref):
    size = hot_ref.shape[0]
    sources, _, width = got_ref.shape
    per = size // 8
    for pair in range(2):
        for g in range(sources // 8):
            part = got_ref[g * 8 : (g + 1) * 8, pair * (size // 8) : (pair + 1) * (size // 8), :]
            rows = dot(hot_ref[...], part.reshape(size, width)).astype(BF16)
            for j in range(8):
                at = (pair * 2 + j // 4) * sources * CAPACITY + g * per
                out_ref[at : at + per, j % 4 * width : (j % 4 + 1) * width] = rows[
                    j * per : (j + 1) * per
                ]


def unroute(hot, got):
    sources, rows, width = got.shape
    vm = pl.BlockSpec(memory_space=pltpu.VMEM)
    return pl.pallas_call(
        unroute_kernel,
        out_shape=struct((sources * rows // 4, width * 4)),
        in_specs=[vm] * 2,
        out_specs=vm,
        compiler_params=params(32),
        cost_estimate=cost(3_400_000_000, 11 << 20),
        name="unroute",
    )(hot, got)


def norm_kernel(me_ref, a0, a1, a2, a3, resid_ref, gain_ref, tgt_ref, mixed_ref, *sends):
    width = a0.shape[1]
    for r, a in enumerate((a0, a1, a2, a3)):
        cols = pl.ds(pl.multiple_of(((me_ref[0] + r) % 4) * width, width), width)
        mixed_ref[:, cols] = resid_ref[0, :, cols].astype(F32) + a[...].astype(F32)
    mixed = mixed_ref[...]
    inv = lax.rsqrt(jnp.mean(mixed * mixed, axis=-1, keepdims=True) + EPS)
    normed = (mixed * inv * gain_ref[...]).astype(BF16)
    part = sends[0].shape[1]
    for i, send in enumerate(sends):
        parts = [normed[:, (i * 4 + q) * part : (i * 4 + q + 1) * part] for q in range(4)]
        place_rows(send, tgt_ref[...], parts)


def norm(me, att, resid, gain, tgt, owners):
    tokens, model = resid.shape[1], resid.shape[2]
    vm = pl.BlockSpec(memory_space=pltpu.VMEM)
    return pl.pallas_call(
        norm_kernel,
        out_shape=[struct((tokens, model), F32)]
        + [struct((owners * 4 * CAPACITY, model // 8))] * 2,
        in_specs=[pl.BlockSpec(memory_space=pltpu.SMEM)] + [vm] * 7,
        out_specs=[vm] * 3,
        compiler_params=params(20),
        cost_estimate=cost(700_000_000, 4 << 20),
        name="norm",
    )(me, *att, resid, gain, tgt)


def regroup(groups):
    size = 8 * groups * CAPACITY
    row = lax.broadcasted_iota(jnp.int32, (size, size), 0)
    col = lax.broadcasted_iota(jnp.int32, (size, size), 1)
    per = 8 * CAPACITY
    group, rest = row // per, row % per
    want = (rest // CAPACITY) * (groups * CAPACITY) + group * CAPACITY + rest % CAPACITY
    return jnp.where(col == want, 1.0, 0.0).astype(BF16)


def unpack_kernel(hot_ref, got_ref, out):
    size = hot_ref.shape[0]
    per, width = size // 4, got_ref.shape[1]
    for g in range(got_ref.shape[0] // size):
        rows = dot(hot_ref[...], got_ref[g * size : (g + 1) * size, :]).astype(BF16)
        for q in range(4):
            out[g * per : (g + 1) * per, q * width : (q + 1) * width] = rows[
                q * per : (q + 1) * per
            ]


def unpack(hot, got):
    rows, width = got.shape
    vm = pl.BlockSpec(memory_space=pltpu.VMEM)
    return pl.pallas_call(
        unpack_kernel,
        out_shape=struct((rows // 4, width * 4)),
        in_specs=[vm] * 2,
        out_specs=vm,
        compiler_params=params(14),
        cost_estimate=cost(1000, 1 << 10),
        name="unpack",
    )(hot, got)


def pack_kernel(hot_ref, o0, o1, f0, f1, g0, g1, send_ref):
    size = hot_ref.shape[0]
    per, width = size // 4, send_ref.shape[1]
    for g in range(send_ref.shape[0] // size):
        at = slice(g * per, (g + 1) * per)
        stack = []
        for own, prev, after in ((o0, f0, g0), (o1, f1, g1)):
            total = own[at, :].astype(F32) + prev[at, :].astype(F32) + after[at, :].astype(F32)
            total = total.astype(BF16)
            stack += [total[:, :width], total[:, width:]]
        send_ref[g * size : (g + 1) * size, :] = dot(
            hot_ref[...], jnp.concatenate(stack, 0), 0, 0
        ).astype(BF16)


def pack(hot, sums):
    rows, width = sums[0].shape
    vm = pl.BlockSpec(memory_space=pltpu.VMEM)
    return pl.pallas_call(
        pack_kernel,
        out_shape=struct((rows * 4, width // 2)),
        in_specs=[vm] * 7,
        out_specs=vm,
        compiler_params=params(20),
        cost_estimate=cost(420_000_000, 6 << 20),
        name="pack",
    )(hot, *sums)


def final_kernel(tgt_ref, mixed_ref, got_ref, out_ref):
    tgt = tgt_ref[...]
    tokens, width = tgt.shape[1], got_ref.shape[1]
    row = lax.broadcasted_iota(jnp.int32, (got_ref.shape[0], tokens), 0)
    got = got_ref[...]
    for q in range(4):
        hot = jnp.where(row == tgt + q * CAPACITY, 1.0, 0.0).astype(BF16)
        cols = slice(q * width, (q + 1) * width)
        out_ref[0, :, cols] = (mixed_ref[:, cols] + dot(hot, got, 0, 0)).astype(BF16)


def final(tgt, mixed, got):
    vm = pl.BlockSpec(memory_space=pltpu.VMEM)
    return pl.pallas_call(
        final_kernel,
        out_shape=struct((1,) + mixed.shape),
        in_specs=[vm] * 3,
        out_specs=vm,
        compiler_params=params(16),
        cost_estimate=cost(700_000_000, 3 << 20),
        name="combine",
    )(tgt, mixed, got)


def forward(x0, x1, w_in, w_out):
    width = x0.shape[1]
    pre = dot(x0, w_in[:width]) + dot(x1, w_in[width:])
    hidden = jax.nn.gelu(pre).astype(BF16)
    return pre, hidden, dot(hidden, w_out).astype(BF16)


def backward(pre, back):
    pull = jax.vjp(jax.nn.gelu, pre)[1]
    return pull(back)[0].astype(BF16)


def slopes(pres, back):
    rows = pres[0].shape[0]
    return [backward(pre, back[i * rows : (i + 1) * rows]) for i, pre in enumerate(pres)]


def stack_rows(*columns):
    rows = sum(x.shape[0] for x in columns[0])
    width = columns[0][0].shape[1]

    def kernel(*refs):
        out, refs = refs[-1], list(refs[:-1])
        for c, column in enumerate(columns):
            at = 0
            for x in column:
                out[at : at + x.shape[0], c * width : (c + 1) * width] = refs.pop(0)[...]
                at += x.shape[0]

    vm = pl.BlockSpec(memory_space=pltpu.VMEM)
    flat = [x for column in columns for x in column]
    return pl.pallas_call(
        kernel,
        out_shape=struct((rows, width * len(columns))),
        in_specs=[vm] * len(flat),
        out_specs=vm,
        compiler_params=params(24),
        cost_estimate=cost(0, 4 * rows * width * len(columns)),
        name="stack_rows",
    )(*flat)


def shards(queries, keys, values, resid, cotangent, zone_ids, norm_gain, w_in, w_out):
    model = queries.shape[2]
    owners = lax.axis_size("seq") * lax.axis_size("expert")
    seq_at = lax.axis_index("seq").astype(jnp.int32).reshape(1)
    dp_at = lax.axis_index("dp").astype(jnp.int32)

    def exchange(blocks):
        shaped = blocks.reshape(owners, 4 * CAPACITY, -1)
        return lax.all_to_all(shaped, ("seq", "expert"), 0, 0, tiled=True)

    def flat(blocks):
        return blocks.reshape(-1, blocks.shape[-1])

    hot, hot_pair = regroup(4), regroup(8)
    zone_row = zone_ids[:, :, 0]
    tgt = slots(zone_row, owners)
    g_planes = lax.all_gather(cotangent, "dp", axis=0, tiled=True)
    zones = jnp.stack([zone_row] + [shift(zone_row, "dp", r) for r in (1, -1, 2)])
    order = jnp.stack([(dp_at + r) % 4 for r in (0, 3, 1, 2)])

    sent = split_heads(seq_at, queries, keys, values)
    pieces = [sent[0]] + [shift(sent[r], "seq", r) for r in (1, 2, 3)]
    att = attention(pieces, model // HEADS)
    att = [att[0]] + [shift(att[r], "seq", -r) for r in (1, 2, 3)]
    mixed, send0, send1 = norm(seq_at, att, resid, norm_gain.reshape(1, model), tgt, owners)
    send_g = route(order, zones, g_planes, owners)
    got0, send_g = lax.optimization_barrier((exchange(send0), send_g))
    x0 = unpack(hot, flat(got0))
    p0, n0 = shift(x0, "dp", 1), shift(x0, "dp", -1)
    send1, _ = lax.optimization_barrier((send1, x0))
    got1 = exchange(send1)
    x1 = unpack(hot, flat(got1))
    p1, n1 = shift(x1, "dp", 1), shift(x1, "dp", -1)
    send_g, _ = lax.optimization_barrier((send_g, got1))
    got_g = lax.all_to_all(send_g, ("seq", "expert"), 0, 0, tiled=True)

    w_first, w_second = w_in[0], w_out[0]
    width = model // 2
    own_pre, own_h, own = forward(x0, x1, w_first, w_second)
    p0, p1, n0, n1, own, own_h, own_pre = lax.optimization_barrier(
        (p0, p1, n0, n1, own, own_h, own_pre)
    )
    far0, far1 = shift(p0, "dp", 1), shift(n1, "dp", -1)
    prev_pre, prev_h, prev = forward(p0, p1, w_first, w_second)
    next_pre, next_h, after = forward(n0, n1, w_first, w_second)
    to_prev0 = shift(prev[:, :width], "dp", -1)
    to_next1 = shift(after[:, width:], "dp", 1)
    far0, far1, prev, after, prev_pre, next_pre, prev_h, next_h = lax.optimization_barrier(
        (far0, far1, prev, after, prev_pre, next_pre, prev_h, next_h)
    )
    far_pre, far_h, far = forward(far0, far1, w_first, w_second)
    via0, via1 = shift(far[:, :width], "dp", 1), shift(far[:, width:], "dp", -1)
    far0, far1, _ = lax.optimization_barrier((far0, far1, far))
    x_rows = stack_rows([x0, p0, n0, far0], [x1, p1, n1, far1])
    h_rows = stack_rows([own_h, prev_h, next_h, far_h])
    via0, via1, x_rows, h_rows = lax.optimization_barrier((via0, via1, x_rows, h_rows))
    sum0 = (after[:, :width].astype(F32) + via0.astype(F32)).astype(BF16)
    sum1 = (prev[:, width:].astype(F32) + via1.astype(F32)).astype(BF16)
    to_next0, to_prev1 = shift(sum0, "dp", 1), shift(sum1, "dp", -1)
    got_g, _, _ = lax.optimization_barrier((got_g, sum0, sum1))
    g_rows = unroute(hot_pair, got_g)
    back = dot(g_rows, w_second, 1, 1)
    sums = [own[:, :width], own[:, width:], to_next0, to_next1, to_prev0, to_prev1]
    *sums, back = lax.optimization_barrier((*sums, back))
    packed, back, g_rows = lax.optimization_barrier((pack(hot, sums), back, g_rows))
    d_rows = stack_rows(slopes((own_pre, prev_pre, next_pre, far_pre), back))
    first = dot(x_rows, d_rows, 0, 0).astype(BF16)
    second = dot(h_rows, g_rows, 0, 0).astype(BF16)
    layer_out = final(tgt, mixed, flat(exchange(packed)))
    return (layer_out, first[None], second[None])


def solution(mesh):
    token = P(("dp", "expert"), "seq", None)
    first = P(("seq", "expert"), None, "dp")
    second = P(("seq", "expert"), "dp", None)
    return jax.shard_map(
        shards,
        mesh=mesh,
        in_specs=(token,) * 6 + (P(), first, second),
        out_specs=(token, first, second),
        check_vma=False,
    )
```

```python
import math

import jax
import jax.numpy as jnp
from jax import lax
from jax.experimental import pallas as pl
from jax.experimental.pallas import tpu as pltpu
from jax.sharding import PartitionSpec as P

HEADS = 16
CAPACITY = 10
EPS = 1e-05
F32 = jnp.float32
BF16 = jnp.bfloat16
MIB = 1 << 20


def params(mib, **kw):
    return pltpu.CompilerParams(vmem_limit_bytes=mib * MIB, **kw)


def cost(flops, nbytes, trans=0):
    return pl.CostEstimate(flops=flops, bytes_accessed=nbytes, transcendentals=trans)


def struct(shape, dtype=BF16):
    return jax.ShapeDtypeStruct(shape, dtype)


def dot(a, b, ca=1, cb=0):
    return lax.dot_general(a, b, (((ca,), (cb,)), ((), ())), preferred_element_type=F32)


def shift(x, axis, step):
    n = lax.axis_size(axis)
    return lax.ppermute(x, axis, [(i, (i + step) % n) for i in range(n)])


def split_kernel(me_ref, q_ref, k_ref, v_ref, *outs):
    width = outs[0].shape[2]
    for r, out in enumerate(outs):
        at = pl.multiple_of(((me_ref[0] + r) % 4) * width, width)
        for i, ref in enumerate((q_ref, k_ref, v_ref)):
            out[i] = ref[0, :, pl.ds(at, width)]


def split_heads(me, q, k, v):
    rows, width = q.shape[1], q.shape[2] // 4
    vm = pl.BlockSpec(memory_space=pltpu.VMEM)
    return pl.pallas_call(
        split_kernel,
        out_shape=[struct((3, rows, width))] * 4,
        in_specs=[pl.BlockSpec(memory_space=pltpu.SMEM), vm, vm, vm],
        out_specs=[vm] * 4,
        compiler_params=params(12),
        cost_estimate=cost(0, 3 << 20),
        name="split_heads",
    )(me, q, k, v)


def attention_kernel(scale, dim, p0, p1, p2, p3, o0, o1, o2, o3):
    pieces, outs = (p0, p1, p2, p3), (o0, o1, o2, o3)
    rows = p0.shape[1]
    for h in range(p0.shape[2] // dim):
        cols = slice(h * dim, (h + 1) * dim)
        k = jnp.concatenate([p[1, :, cols] for p in pieces], 0)
        v = jnp.concatenate([p[2, :, cols] for p in pieces], 0)
        q = jnp.concatenate([p[0, :, cols] for p in pieces], 0)
        scores = dot(q, k, 1, 1) * scale
        weights = jnp.exp(scores - jnp.max(scores, axis=-1, keepdims=True))
        totals = jnp.sum(weights, axis=-1, keepdims=True)
        res = dot(weights.astype(BF16), v) / totals
        for i, o in enumerate(outs):
            o[:, cols] = res[i * rows : (i + 1) * rows].astype(BF16)


def attention(pieces, dim):
    _, rows, width = pieces[0].shape
    vm = pl.BlockSpec(memory_space=pltpu.VMEM)
    scale = 1.0 / math.sqrt(dim)
    return pl.pallas_call(
        lambda *refs: attention_kernel(scale, dim, *refs),
        out_shape=[struct((rows, width))] * 4,
        in_specs=[vm] * 4,
        out_specs=[vm] * 4,
        compiler_params=params(28),
        cost_estimate=cost(16 * rows * rows * width * 4, 2 << 20, 1 << 20),
        name="attention",
    )(*pieces)


def place_rows(send_ref, tgt, parts):
    tokens = tgt.shape[1]
    chunk = send_ref.shape[0] // 4
    for c in range(4):
        row = lax.broadcasted_iota(jnp.int32, (chunk, tokens), 0) + c * chunk
        acc = None
        for q, part in enumerate(parts):
            hot = jnp.where(row == tgt + q * CAPACITY, 1.0, 0.0).astype(BF16)
            term = dot(hot, part)
            acc = term if acc is None else acc + term
        send_ref[c * chunk : (c + 1) * chunk, :] = acc.astype(BF16)


def slots_of(zone, owners):
    tokens = zone.shape[1]
    hot = jnp.where(lax.broadcasted_iota(jnp.int32, (owners, tokens), 0) == zone, 1.0, 0.0)
    upper = jnp.where(
        lax.broadcasted_iota(jnp.int32, (tokens, tokens), 0)
        <= lax.broadcasted_iota(jnp.int32, (tokens, tokens), 1),
        1.0,
        0.0,
    )
    rank = dot(hot.astype(BF16), upper.astype(BF16))
    slot = jnp.sum(hot * rank, axis=0, keepdims=True) - 1.0
    return zone * (4 * CAPACITY) + slot.astype(jnp.int32)


def slots(zone_row, owners):
    def kernel(zone_ref, tgt_ref):
        tgt_ref[...] = slots_of(zone_ref[...], owners)

    vm = pl.BlockSpec(memory_space=pltpu.VMEM)
    return pl.pallas_call(
        kernel,
        out_shape=struct(zone_row.shape, jnp.int32),
        in_specs=[vm],
        out_specs=vm,
        compiler_params=params(4),
        cost_estimate=cost(1_000_000, 1000),
        name="slots",
    )(zone_row)


def route_kernel(owners, order_ref, zone_ref, g_ref, send_ref):
    width = send_ref.shape[2]
    block = 4 * CAPACITY
    rows = 8 * block
    for pair in range(2):
        tgts = [slots_of(zone_ref[pair * 2 + j], owners) for j in range(2)]
        for c in range(owners // 8):
            got = []
            for j in range(2):
                row = lax.broadcasted_iota(jnp.int32, (rows, tgts[j].shape[1]), 0) + c * rows
                acc = None
                for q in range(4):
                    hot = jnp.where(row == tgts[j] + q * CAPACITY, 1.0, 0.0).astype(BF16)
                    plane = order_ref[pair * 2 + j]
                    term = dot(hot, g_ref[plane, :, q * width : (q + 1) * width])
                    acc = term if acc is None else acc + term
                got.append(acc.reshape(8, block, width))
            both = jnp.concatenate(got, 1).astype(BF16)
            send_ref[c * 8 : (c + 1) * 8, pair * 2 * block : (pair + 1) * 2 * block, :] = both


def route(order, zones, g_planes, owners):
    model = g_planes.shape[2]
    vm = pl.BlockSpec(memory_space=pltpu.VMEM)
    return pl.pallas_call(
        lambda *refs: route_kernel(owners, *refs),
        out_shape=struct((owners, 16 * CAPACITY, model // 4)),
        in_specs=[pl.BlockSpec(memory_space=pltpu.SMEM), vm, vm],
        out_specs=vm,
        compiler_params=params(32),
        cost_estimate=cost(2_700_000_000, 8 << 20),
        name="route",
    )(order, zones, g_planes)


def unroute_kernel(hot_ref, got_ref, out_ref):
    size = hot_ref.shape[0]
    sources, _, width = got_ref.shape
    per = size // 8
    for pair in range(2):
        for g in range(sources // 8):
            part = got_ref[g * 8 : (g + 1) * 8, pair * 2 * per : (pair + 1) * 2 * per, :]
            part = part.reshape(2 * size, width)
            halves = [dot(hot_ref[...], part[i * size : (i + 1) * size]) for i in range(2)]
            for j in range(8):
                at = (pair * 2 + j // 4) * sources * CAPACITY + g * 2 * per
                rows = jnp.concatenate([h[j * per : (j + 1) * per] for h in halves], 0)
                out_ref[at : at + 2 * per, j % 4 * width : (j % 4 + 1) * width] = rows.astype(BF16)


def unroute(hot, got):
    sources, rows, width = got.shape
    vm = pl.BlockSpec(memory_space=pltpu.VMEM)
    return pl.pallas_call(
        unroute_kernel,
        out_shape=struct((sources * rows // 4, width * 4)),
        in_specs=[vm] * 2,
        out_specs=vm,
        compiler_params=params(32),
        cost_estimate=cost(3_400_000_000, 11 << 20),
        name="unroute",
    )(hot, got)


def norm_kernel(me_ref, a0, a1, a2, a3, resid_ref, gain_ref, tgt_ref, mixed_ref, *sends):
    width = a0.shape[1]
    for r, a in enumerate((a0, a1, a2, a3)):
        cols = pl.ds(pl.multiple_of(((me_ref[0] + r) % 4) * width, width), width)
        mixed_ref[:, cols] = resid_ref[0, :, cols].astype(F32) + a[...].astype(F32)
    mixed = mixed_ref[...]
    inv = lax.rsqrt(jnp.mean(mixed * mixed, axis=-1, keepdims=True) + EPS)
    normed = (mixed * inv * gain_ref[...]).astype(BF16)
    part = sends[0].shape[1]
    for i, send in enumerate(sends):
        parts = [normed[:, (i * 4 + q) * part : (i * 4 + q + 1) * part] for q in range(4)]
        place_rows(send, tgt_ref[...], parts)


def norm(me, att, resid, gain, tgt, owners):
    tokens, model = resid.shape[1], resid.shape[2]
    vm = pl.BlockSpec(memory_space=pltpu.VMEM)
    return pl.pallas_call(
        norm_kernel,
        out_shape=[struct((tokens, model), F32)]
        + [struct((owners * 4 * CAPACITY, model // 8))] * 2,
        in_specs=[pl.BlockSpec(memory_space=pltpu.SMEM)] + [vm] * 7,
        out_specs=[vm] * 3,
        compiler_params=params(20),
        cost_estimate=cost(700_000_000, 4 << 20),
        name="norm",
    )(me, *att, resid, gain, tgt)


def regroup(groups, sources=8):
    size = sources * groups * CAPACITY
    row = lax.broadcasted_iota(jnp.int32, (size, size), 0)
    col = lax.broadcasted_iota(jnp.int32, (size, size), 1)
    per = sources * CAPACITY
    group, rest = row // per, row % per
    want = (rest // CAPACITY) * (groups * CAPACITY) + group * CAPACITY + rest % CAPACITY
    return jnp.where(col == want, 1.0, 0.0).astype(BF16)


def unpack_kernel(hot_ref, got_ref, out):
    size = hot_ref.shape[0]
    per, width = size // 4, got_ref.shape[1]
    for g in range(got_ref.shape[0] // size):
        rows = dot(hot_ref[...], got_ref[g * size : (g + 1) * size, :]).astype(BF16)
        for q in range(4):
            out[g * per : (g + 1) * per, q * width : (q + 1) * width] = rows[
                q * per : (q + 1) * per
            ]


def unpack(hot, got):
    rows, width = got.shape
    vm = pl.BlockSpec(memory_space=pltpu.VMEM)
    return pl.pallas_call(
        unpack_kernel,
        out_shape=struct((rows // 4, width * 4)),
        in_specs=[vm] * 2,
        out_specs=vm,
        compiler_params=params(14),
        cost_estimate=cost(1000, 1 << 10),
        name="unpack",
    )(hot, got)


def pack_kernel(hot_ref, o0, o1, f0, f1, g0, g1, send_ref):
    size = hot_ref.shape[0]
    per, width = size // 4, send_ref.shape[1]
    for g in range(send_ref.shape[0] // size):
        at = slice(g * per, (g + 1) * per)
        stack = []
        for own, prev, after in ((o0, f0, g0), (o1, f1, g1)):
            total = own[at, :].astype(F32) + prev[at, :].astype(F32) + after[at, :].astype(F32)
            total = total.astype(BF16)
            stack += [total[:, :width], total[:, width:]]
        send_ref[g * size : (g + 1) * size, :] = dot(
            hot_ref[...], jnp.concatenate(stack, 0), 0, 0
        ).astype(BF16)


def pack(hot, sums):
    rows, width = sums[0].shape
    vm = pl.BlockSpec(memory_space=pltpu.VMEM)
    return pl.pallas_call(
        pack_kernel,
        out_shape=struct((rows * 4, width // 2)),
        in_specs=[vm] * 7,
        out_specs=vm,
        compiler_params=params(60),
        cost_estimate=cost(420_000_000, 6 << 20),
        name="pack",
    )(hot, *sums)


def final_kernel(tgt_ref, mixed_ref, got_ref, out_ref):
    tgt = tgt_ref[...]
    tokens, width = tgt.shape[1], got_ref.shape[1]
    row = lax.broadcasted_iota(jnp.int32, (got_ref.shape[0], tokens), 0)
    got = got_ref[...]
    for q in range(4):
        hot = jnp.where(row == tgt + q * CAPACITY, 1.0, 0.0).astype(BF16)
        cols = slice(q * width, (q + 1) * width)
        out_ref[0, :, cols] = (mixed_ref[:, cols] + dot(hot, got, 0, 0)).astype(BF16)


def final(tgt, mixed, got):
    vm = pl.BlockSpec(memory_space=pltpu.VMEM)
    return pl.pallas_call(
        final_kernel,
        out_shape=struct((1,) + mixed.shape),
        in_specs=[vm] * 3,
        out_specs=vm,
        compiler_params=params(16),
        cost_estimate=cost(700_000_000, 3 << 20),
        name="combine",
    )(tgt, mixed, got)


def forward(x0, x1, w_in, w_out):
    width = x0.shape[1]
    pre = dot(x0, w_in[:width]) + dot(x1, w_in[width:])
    act, pull = jax.vjp(jax.nn.gelu, pre)
    hidden = act.astype(BF16)
    return pull(jnp.ones_like(pre))[0], hidden, dot(hidden, w_out).astype(BF16)


def stack_rows(*columns):
    rows = sum(x.shape[0] for x in columns[0])
    width = columns[0][0].shape[1]

    def kernel(*refs):
        out, refs = refs[-1], list(refs[:-1])
        for c, column in enumerate(columns):
            at = 0
            for x in column:
                out[at : at + x.shape[0], c * width : (c + 1) * width] = refs.pop(0)[...]
                at += x.shape[0]

    vm = pl.BlockSpec(memory_space=pltpu.VMEM)
    flat = [x for column in columns for x in column]
    return pl.pallas_call(
        kernel,
        out_shape=struct((rows, width * len(columns)), flat[0].dtype),
        in_specs=[vm] * len(flat),
        out_specs=vm,
        compiler_params=params(24),
        cost_estimate=cost(0, 4 * rows * width * len(columns)),
        name="stack_rows",
    )(*flat)


def turned_rows(*columns):
    rows = sum(x.shape[0] for x in columns[0])
    width = columns[0][0].shape[1]
    step = 256

    def kernel(*refs):
        out, stacked, refs = refs[-2], refs[-1], list(refs[:-2])
        for c, column in enumerate(columns):
            at = 0
            for x in column:
                stacked[at : at + x.shape[0], :] = refs.pop(0)[...]
                at += x.shape[0]
            for k in range(0, width, step):
                out[c * width + k : c * width + k + step, :] = stacked[:, k : k + step].T

    vm = pl.BlockSpec(memory_space=pltpu.VMEM)
    flat = [x for column in columns for x in column]
    return pl.pallas_call(
        kernel,
        out_shape=struct((width * len(columns), rows)),
        in_specs=[vm] * len(flat),
        out_specs=vm,
        scratch_shapes=[pltpu.VMEM((rows, width), BF16)],
        compiler_params=params(40),
        cost_estimate=cost(0, 4 * rows * width * len(columns)),
        name="turned_rows",
    )(*flat)


def shards(queries, keys, values, resid, cotangent, zone_ids, norm_gain, w_in, w_out):
    model = queries.shape[2]
    owners = lax.axis_size("seq") * lax.axis_size("expert")
    seq_at = lax.axis_index("seq").astype(jnp.int32).reshape(1)
    dp_at = lax.axis_index("dp").astype(jnp.int32)

    def exchange(blocks):
        shaped = blocks.reshape(owners, 4 * CAPACITY, -1)
        return lax.all_to_all(shaped, ("seq", "expert"), 0, 0, tiled=True)

    def flat(blocks):
        return blocks.reshape(-1, blocks.shape[-1])

    hot, hot_pair = regroup(4), regroup(8, 4)
    zone_row = zone_ids[:, :, 0]
    tgt = slots(zone_row, owners)
    g_planes = lax.all_gather(cotangent, "dp", axis=0, tiled=True)
    zones = jnp.stack([zone_row] + [shift(zone_row, "dp", r) for r in (1, -1, 2)])
    order = jnp.stack([(dp_at + r) % 4 for r in (0, 3, 1, 2)])

    sent = split_heads(seq_at, queries, keys, values)
    pieces = [sent[0]] + [shift(sent[r], "seq", r) for r in (1, 2, 3)]
    att = attention(pieces, model // HEADS)
    att = [att[0]] + [shift(att[r], "seq", -r) for r in (1, 2, 3)]
    mixed, send0, send1 = norm(seq_at, att, resid, norm_gain.reshape(1, model), tgt, owners)
    send_g = route(order, zones, g_planes, owners)
    got0, send_g = lax.optimization_barrier((exchange(send0), send_g))
    x0 = unpack(hot, flat(got0))
    p0, n0 = shift(x0, "dp", 1), shift(x0, "dp", -1)
    send1, _ = lax.optimization_barrier((send1, x0))
    got1 = exchange(send1)
    x1 = unpack(hot, flat(got1))
    p1, n1 = shift(x1, "dp", 1), shift(x1, "dp", -1)
    send_g, _ = lax.optimization_barrier((send_g, got1))
    got_g = lax.all_to_all(send_g, ("seq", "expert"), 0, 0, tiled=True)

    w_first, w_second = w_in[0], w_out[0]
    width = model // 2
    own_s, own_h, own = forward(x0, x1, w_first, w_second)
    p0, p1, n0, n1, own, own_h, own_s = lax.optimization_barrier(
        (p0, p1, n0, n1, own, own_h, own_s)
    )
    far0, far1 = shift(p0, "dp", 1), shift(n1, "dp", -1)
    prev_s, prev_h, prev = forward(p0, p1, w_first, w_second)
    next_s, next_h, after = forward(n0, n1, w_first, w_second)
    to_prev0 = shift(prev[:, :width], "dp", -1)
    to_next1 = shift(after[:, width:], "dp", 1)
    far0, far1, prev, after, prev_s, next_s, prev_h, next_h = lax.optimization_barrier(
        (far0, far1, prev, after, prev_s, next_s, prev_h, next_h)
    )
    far_s, far_h, far = forward(far0, far1, w_first, w_second)
    via0, via1 = shift(far[:, :width], "dp", 1), shift(far[:, width:], "dp", -1)
    far0, far1, _ = lax.optimization_barrier((far0, far1, far))
    x_rows = turned_rows([x0, p0, n0, far0], [x1, p1, n1, far1])
    h_rows = turned_rows([own_h, prev_h, next_h, far_h])
    slope_rows = stack_rows([own_s, prev_s, next_s, far_s])
    via0, via1, x_rows, h_rows, slope_rows = lax.optimization_barrier(
        (via0, via1, x_rows, h_rows, slope_rows)
    )
    sum0 = (after[:, :width].astype(F32) + via0.astype(F32)).astype(BF16)
    sum1 = (prev[:, width:].astype(F32) + via1.astype(F32)).astype(BF16)
    to_next0, to_prev1 = shift(sum0, "dp", 1), shift(sum1, "dp", -1)
    got_g, _, _ = lax.optimization_barrier((got_g, sum0, sum1))
    g_rows = unroute(hot_pair, got_g)
    d_rows = (dot(g_rows, w_second, 1, 1) * slope_rows).astype(BF16)
    sums = [own[:, :width], own[:, width:], to_next0, to_next1, to_prev0, to_prev1]
    *sums, d_rows = lax.optimization_barrier((*sums, d_rows))
    packed, d_rows, g_rows = lax.optimization_barrier((pack(hot, sums), d_rows, g_rows))
    first = dot(x_rows, d_rows).astype(BF16)
    second = dot(h_rows, g_rows).astype(BF16)
    layer_out = final(tgt, mixed, flat(exchange(packed)))
    return (layer_out, first[None], second[None])


def solution(mesh):
    token = P(("dp", "expert"), "seq", None)
    first = P(("seq", "expert"), None, "dp")
    second = P(("seq", "expert"), "dp", None)
    return jax.shard_map(
        shards,
        mesh=mesh,
        in_specs=(token,) * 6 + (P(), first, second),
        out_specs=(token, first, second),
        check_vma=False,
    )
```

```python
import math

import jax
import jax.numpy as jnp
from jax import lax
from jax.experimental import pallas as pl
from jax.experimental.pallas import tpu as pltpu
from jax.sharding import PartitionSpec as P

HEADS = 16
CAPACITY = 10
EPS = 1e-05
F32 = jnp.float32
BF16 = jnp.bfloat16
MIB = 1 << 20


def params(mib, **kw):
    return pltpu.CompilerParams(vmem_limit_bytes=mib * MIB, **kw)


def cost(flops, nbytes, trans=0):
    return pl.CostEstimate(flops=flops, bytes_accessed=nbytes, transcendentals=trans)


def struct(shape, dtype=BF16):
    return jax.ShapeDtypeStruct(shape, dtype)


def dot(a, b, ca=1, cb=0):
    return lax.dot_general(a, b, (((ca,), (cb,)), ((), ())), preferred_element_type=F32)


def shift(x, axis, step):
    n = lax.axis_size(axis)
    return lax.ppermute(x, axis, [(i, (i + step) % n) for i in range(n)])


def split_kernel(me_ref, q_ref, k_ref, v_ref, *outs):
    width = outs[0].shape[2]
    for r, out in enumerate(outs):
        at = pl.multiple_of(((me_ref[0] + r) % 4) * width, width)
        for i, ref in enumerate((q_ref, k_ref, v_ref)):
            out[i] = ref[0, :, pl.ds(at, width)]


def split_heads(me, q, k, v):
    rows, width = q.shape[1], q.shape[2] // 4
    vm = pl.BlockSpec(memory_space=pltpu.VMEM)
    return pl.pallas_call(
        split_kernel,
        out_shape=[struct((3, rows, width))] * 4,
        in_specs=[pl.BlockSpec(memory_space=pltpu.SMEM), vm, vm, vm],
        out_specs=[vm] * 4,
        compiler_params=params(12),
        cost_estimate=cost(0, 3 << 20),
        name="split_heads",
    )(me, q, k, v)


def attention_kernel(scale, dim, p0, p1, p2, p3, o0, o1, o2, o3):
    pieces, outs = (p0, p1, p2, p3), (o0, o1, o2, o3)
    rows = p0.shape[1]
    for h in range(p0.shape[2] // dim):
        cols = slice(h * dim, (h + 1) * dim)
        k = jnp.concatenate([p[1, :, cols] for p in pieces], 0)
        v = jnp.concatenate([p[2, :, cols] for p in pieces], 0)
        q = jnp.concatenate([p[0, :, cols] for p in pieces], 0)
        scores = dot(q, k, 1, 1) * scale
        weights = jnp.exp(scores - jnp.max(scores, axis=-1, keepdims=True))
        totals = jnp.sum(weights, axis=-1, keepdims=True)
        res = dot(weights.astype(BF16), v) / totals
        for i, o in enumerate(outs):
            o[:, cols] = res[i * rows : (i + 1) * rows].astype(BF16)


def attention(pieces, dim):
    _, rows, width = pieces[0].shape
    vm = pl.BlockSpec(memory_space=pltpu.VMEM)
    scale = 1.0 / math.sqrt(dim)
    return pl.pallas_call(
        lambda *refs: attention_kernel(scale, dim, *refs),
        out_shape=[struct((rows, width))] * 4,
        in_specs=[vm] * 4,
        out_specs=[vm] * 4,
        compiler_params=params(28),
        cost_estimate=cost(16 * rows * rows * width * 4, 2 << 20, 1 << 20),
        name="attention",
    )(*pieces)


def place_rows(send_ref, tgt, parts):
    tokens = tgt.shape[1]
    chunk = send_ref.shape[0] // 4
    for c in range(4):
        row = lax.broadcasted_iota(jnp.int32, (chunk, tokens), 0) + c * chunk
        acc = None
        for q, part in enumerate(parts):
            hot = jnp.where(row == tgt + q * CAPACITY, 1.0, 0.0).astype(BF16)
            term = dot(hot, part)
            acc = term if acc is None else acc + term
        send_ref[c * chunk : (c + 1) * chunk, :] = acc.astype(BF16)


def slots_of(zone, owners):
    tokens = zone.shape[1]
    hot = jnp.where(lax.broadcasted_iota(jnp.int32, (owners, tokens), 0) == zone, 1.0, 0.0)
    upper = jnp.where(
        lax.broadcasted_iota(jnp.int32, (tokens, tokens), 0)
        <= lax.broadcasted_iota(jnp.int32, (tokens, tokens), 1),
        1.0,
        0.0,
    )
    rank = dot(hot.astype(BF16), upper.astype(BF16))
    slot = jnp.sum(hot * rank, axis=0, keepdims=True) - 1.0
    return zone * (4 * CAPACITY) + slot.astype(jnp.int32)


def slots(zone_row, owners):
    def kernel(zone_ref, tgt_ref):
        tgt_ref[...] = slots_of(zone_ref[...], owners)

    vm = pl.BlockSpec(memory_space=pltpu.VMEM)
    return pl.pallas_call(
        kernel,
        out_shape=struct(zone_row.shape, jnp.int32),
        in_specs=[vm],
        out_specs=vm,
        compiler_params=params(4),
        cost_estimate=cost(1_000_000, 1000),
        name="slots",
    )(zone_row)


def route_kernel(owners, order_ref, zone_ref, g_ref, send_ref):
    width = send_ref.shape[2]
    block = 4 * CAPACITY
    rows = 8 * block
    for pair in range(2):
        tgts = [slots_of(zone_ref[pair * 2 + j], owners) for j in range(2)]
        for c in range(owners // 8):
            got = []
            for j in range(2):
                row = lax.broadcasted_iota(jnp.int32, (rows, tgts[j].shape[1]), 0) + c * rows
                acc = None
                for q in range(4):
                    hot = jnp.where(row == tgts[j] + q * CAPACITY, 1.0, 0.0).astype(BF16)
                    plane = order_ref[pair * 2 + j]
                    term = dot(hot, g_ref[plane, :, q * width : (q + 1) * width])
                    acc = term if acc is None else acc + term
                got.append(acc.reshape(8, block, width))
            both = jnp.concatenate(got, 1).astype(BF16)
            send_ref[c * 8 : (c + 1) * 8, pair * 2 * block : (pair + 1) * 2 * block, :] = both


def route(order, zones, g_planes, owners):
    model = g_planes.shape[2]
    vm = pl.BlockSpec(memory_space=pltpu.VMEM)
    return pl.pallas_call(
        lambda *refs: route_kernel(owners, *refs),
        out_shape=struct((owners, 16 * CAPACITY, model // 4)),
        in_specs=[pl.BlockSpec(memory_space=pltpu.SMEM), vm, vm],
        out_specs=vm,
        compiler_params=params(32),
        cost_estimate=cost(2_700_000_000, 8 << 20),
        name="route",
    )(order, zones, g_planes)


def unroute_kernel(hot_ref, got_ref, out_ref):
    size = hot_ref.shape[0]
    sources, _, width = got_ref.shape
    per = size // 8
    for pair in range(2):
        for g in range(sources // 8):
            part = got_ref[g * 8 : (g + 1) * 8, pair * 2 * per : (pair + 1) * 2 * per, :]
            part = part.reshape(2 * size, width)
            halves = [dot(hot_ref[...], part[i * size : (i + 1) * size]) for i in range(2)]
            for j in range(8):
                at = (pair * 2 + j // 4) * sources * CAPACITY + g * 2 * per
                rows = jnp.concatenate([h[j * per : (j + 1) * per] for h in halves], 0)
                out_ref[at : at + 2 * per, j % 4 * width : (j % 4 + 1) * width] = rows.astype(BF16)


def unroute(hot, got):
    sources, rows, width = got.shape
    vm = pl.BlockSpec(memory_space=pltpu.VMEM)
    return pl.pallas_call(
        unroute_kernel,
        out_shape=struct((sources * rows // 4, width * 4)),
        in_specs=[vm] * 2,
        out_specs=vm,
        compiler_params=params(32),
        cost_estimate=cost(3_400_000_000, 11 << 20),
        name="unroute",
    )(hot, got)


def norm_kernel(me_ref, a0, a1, a2, a3, resid_ref, gain_ref, tgt_ref, mixed_ref, *sends):
    width = a0.shape[1]
    for r, a in enumerate((a0, a1, a2, a3)):
        cols = pl.ds(pl.multiple_of(((me_ref[0] + r) % 4) * width, width), width)
        mixed_ref[:, cols] = resid_ref[0, :, cols].astype(F32) + a[...].astype(F32)
    mixed = mixed_ref[...]
    inv = lax.rsqrt(jnp.mean(mixed * mixed, axis=-1, keepdims=True) + EPS)
    normed = (mixed * inv * gain_ref[...]).astype(BF16)
    part = sends[0].shape[1]
    for i, send in enumerate(sends):
        parts = [normed[:, (i * 4 + q) * part : (i * 4 + q + 1) * part] for q in range(4)]
        place_rows(send, tgt_ref[...], parts)


def norm(me, att, resid, gain, tgt, owners):
    tokens, model = resid.shape[1], resid.shape[2]
    vm = pl.BlockSpec(memory_space=pltpu.VMEM)
    return pl.pallas_call(
        norm_kernel,
        out_shape=[struct((tokens, model), F32)]
        + [struct((owners * 4 * CAPACITY, model // 8))] * 2,
        in_specs=[pl.BlockSpec(memory_space=pltpu.SMEM)] + [vm] * 7,
        out_specs=[vm] * 3,
        compiler_params=params(20),
        cost_estimate=cost(700_000_000, 4 << 20),
        name="norm",
    )(me, *att, resid, gain, tgt)


def regroup(groups, sources=8):
    size = sources * groups * CAPACITY
    row = lax.broadcasted_iota(jnp.int32, (size, size), 0)
    col = lax.broadcasted_iota(jnp.int32, (size, size), 1)
    per = sources * CAPACITY
    group, rest = row // per, row % per
    want = (rest // CAPACITY) * (groups * CAPACITY) + group * CAPACITY + rest % CAPACITY
    return jnp.where(col == want, 1.0, 0.0).astype(BF16)


def unpack_kernel(hot_ref, got_ref, out):
    size = hot_ref.shape[0]
    per, width = size // 4, got_ref.shape[1]
    for g in range(got_ref.shape[0] // size):
        rows = dot(hot_ref[...], got_ref[g * size : (g + 1) * size, :]).astype(BF16)
        for q in range(4):
            out[g * per : (g + 1) * per, q * width : (q + 1) * width] = rows[
                q * per : (q + 1) * per
            ]


def unpack(hot, got):
    rows, width = got.shape
    vm = pl.BlockSpec(memory_space=pltpu.VMEM)
    return pl.pallas_call(
        unpack_kernel,
        out_shape=struct((rows // 4, width * 4)),
        in_specs=[vm] * 2,
        out_specs=vm,
        compiler_params=params(14),
        cost_estimate=cost(1000, 1 << 10),
        name="unpack",
    )(hot, got)


def pack_kernel(hot_ref, o0, o1, f0, f1, g0, g1, send_ref):
    size = hot_ref.shape[0]
    per, width = size // 4, send_ref.shape[1]
    for g in range(send_ref.shape[0] // size):
        at = slice(g * per, (g + 1) * per)
        stack = []
        for own, prev, after in ((o0, f0, g0), (o1, f1, g1)):
            total = own[at, :].astype(F32) + prev[at, :].astype(F32) + after[at, :].astype(F32)
            total = total.astype(BF16)
            stack += [total[:, :width], total[:, width:]]
        send_ref[g * size : (g + 1) * size, :] = dot(
            hot_ref[...], jnp.concatenate(stack, 0), 0, 0
        ).astype(BF16)


def pack(hot, sums):
    rows, width = sums[0].shape
    vm = pl.BlockSpec(memory_space=pltpu.VMEM)
    return pl.pallas_call(
        pack_kernel,
        out_shape=struct((rows * 4, width // 2)),
        in_specs=[vm] * 7,
        out_specs=vm,
        compiler_params=params(60),
        cost_estimate=cost(420_000_000, 6 << 20),
        name="pack",
    )(hot, *sums)


def final_kernel(tgt_ref, mixed_ref, got_ref, out_ref):
    tgt = tgt_ref[...]
    tokens, width = tgt.shape[1], got_ref.shape[1]
    row = lax.broadcasted_iota(jnp.int32, (got_ref.shape[0], tokens), 0)
    got = got_ref[...]
    for q in range(4):
        hot = jnp.where(row == tgt + q * CAPACITY, 1.0, 0.0).astype(BF16)
        cols = slice(q * width, (q + 1) * width)
        out_ref[0, :, cols] = (mixed_ref[:, cols] + dot(hot, got, 0, 0)).astype(BF16)


def final(tgt, mixed, got):
    vm = pl.BlockSpec(memory_space=pltpu.VMEM)
    return pl.pallas_call(
        final_kernel,
        out_shape=struct((1,) + mixed.shape),
        in_specs=[vm] * 3,
        out_specs=vm,
        compiler_params=params(16),
        cost_estimate=cost(700_000_000, 3 << 20),
        name="combine",
    )(tgt, mixed, got)


def forward(x0, x1, w_in, w_out):
    width = x0.shape[1]
    pre = dot(x0, w_in[:width]) + dot(x1, w_in[width:])
    act, pull = jax.vjp(jax.nn.gelu, pre)
    hidden = act.astype(BF16)
    return pull(jnp.ones_like(pre))[0], hidden, dot(hidden, w_out).astype(BF16)


def stack_rows(*columns):
    rows = sum(x.shape[0] for x in columns[0])
    width = columns[0][0].shape[1]

    def kernel(*refs):
        out, refs = refs[-1], list(refs[:-1])
        for c, column in enumerate(columns):
            at = 0
            for x in column:
                out[at : at + x.shape[0], c * width : (c + 1) * width] = refs.pop(0)[...]
                at += x.shape[0]

    vm = pl.BlockSpec(memory_space=pltpu.VMEM)
    flat = [x for column in columns for x in column]
    return pl.pallas_call(
        kernel,
        out_shape=struct((rows, width * len(columns)), flat[0].dtype),
        in_specs=[vm] * len(flat),
        out_specs=vm,
        compiler_params=params(24),
        cost_estimate=cost(0, 4 * rows * width * len(columns)),
        name="stack_rows",
    )(*flat)


def turned_rows(*columns):
    rows = sum(x.shape[0] for x in columns[0])
    width = columns[0][0].shape[1]
    step = 256

    def kernel(*refs):
        out, stacked, refs = refs[-2], refs[-1], list(refs[:-2])
        for c, column in enumerate(columns):
            at = 0
            for x in column:
                stacked[at : at + x.shape[0], :] = refs.pop(0)[...]
                at += x.shape[0]
            for k in range(0, width, step):
                out[c * width + k : c * width + k + step, :] = stacked[:, k : k + step].T

    vm = pl.BlockSpec(memory_space=pltpu.VMEM)
    flat = [x for column in columns for x in column]
    return pl.pallas_call(
        kernel,
        out_shape=struct((width * len(columns), rows)),
        in_specs=[vm] * len(flat),
        out_specs=vm,
        scratch_shapes=[pltpu.VMEM((rows, width), BF16)],
        compiler_params=params(40),
        cost_estimate=cost(0, 4 * rows * width * len(columns)),
        name="turned_rows",
    )(*flat)


def shards(queries, keys, values, resid, cotangent, zone_ids, norm_gain, w_in, w_out):
    model = queries.shape[2]
    owners = lax.axis_size("seq") * lax.axis_size("expert")
    seq_at = lax.axis_index("seq").astype(jnp.int32).reshape(1)
    dp_at = lax.axis_index("dp").astype(jnp.int32)

    def exchange(blocks):
        shaped = blocks.reshape(owners, 4 * CAPACITY, -1)
        return lax.all_to_all(shaped, ("seq", "expert"), 0, 0, tiled=True)

    def flat(blocks):
        return blocks.reshape(-1, blocks.shape[-1])

    hot, hot_pair = regroup(4), regroup(8, 4)
    zone_row = zone_ids[:, :, 0]
    tgt = slots(zone_row, owners)
    g_planes = lax.all_gather(cotangent, "dp", axis=0, tiled=True)
    zones = jnp.stack([zone_row] + [shift(zone_row, "dp", r) for r in (1, -1, 2)])
    order = jnp.stack([(dp_at + r) % 4 for r in (0, 3, 1, 2)])

    sent = split_heads(seq_at, queries, keys, values)
    pieces = [sent[0]] + [shift(sent[r], "seq", r) for r in (1, 2, 3)]
    att = attention(pieces, model // HEADS)
    att = [att[0]] + [shift(att[r], "seq", -r) for r in (1, 2, 3)]
    mixed, send0, send1 = norm(seq_at, att, resid, norm_gain.reshape(1, model), tgt, owners)
    send_g = route(order, zones, g_planes, owners)
    got0, send_g = lax.optimization_barrier((exchange(send0), send_g))
    x0 = unpack(hot, flat(got0))
    p0, n0 = shift(x0, "dp", 1), shift(x0, "dp", -1)
    send1, _ = lax.optimization_barrier((send1, x0))
    got1 = exchange(send1)
    x1 = unpack(hot, flat(got1))
    p1, n1 = shift(x1, "dp", 1), shift(x1, "dp", -1)
    send_g, _ = lax.optimization_barrier((send_g, got1))
    got_g = lax.all_to_all(send_g, ("seq", "expert"), 0, 0, tiled=True)

    w_first, w_second = w_in[0], w_out[0]
    width = model // 2
    x0, x1, p0, n0 = lax.optimization_barrier((x0, x1, p0, n0))
    own_s, own_h, own = forward(x0, x1, w_first, w_second)
    p0, p1, n0, n1, own, own_h, own_s = lax.optimization_barrier(
        (p0, p1, n0, n1, own, own_h, own_s)
    )
    far0, far1 = shift(p0, "dp", 1), shift(n1, "dp", -1)
    prev_s, prev_h, prev = forward(p0, p1, w_first, w_second)
    next_s, next_h, after = forward(n0, n1, w_first, w_second)
    to_prev0 = shift(prev[:, :width], "dp", -1)
    to_next1 = shift(after[:, width:], "dp", 1)
    far0, far1, prev, after, prev_s, next_s, prev_h, next_h = lax.optimization_barrier(
        (far0, far1, prev, after, prev_s, next_s, prev_h, next_h)
    )
    far_s, far_h, far = forward(far0, far1, w_first, w_second)
    via0, via1 = shift(far[:, :width], "dp", 1), shift(far[:, width:], "dp", -1)
    far0, far1, _ = lax.optimization_barrier((far0, far1, far))
    x_rows = turned_rows([x0, p0, n0, far0], [x1, p1, n1, far1])
    h_rows = turned_rows([own_h, prev_h, next_h, far_h])
    slope_rows = stack_rows([own_s, prev_s, next_s, far_s])
    via0, via1, x_rows, h_rows, slope_rows = lax.optimization_barrier(
        (via0, via1, x_rows, h_rows, slope_rows)
    )
    sum0 = (after[:, :width].astype(F32) + via0.astype(F32)).astype(BF16)
    sum1 = (prev[:, width:].astype(F32) + via1.astype(F32)).astype(BF16)
    to_next0, to_prev1 = shift(sum0, "dp", 1), shift(sum1, "dp", -1)
    got_g, _, _ = lax.optimization_barrier((got_g, sum0, sum1))
    g_rows = unroute(hot_pair, got_g)
    d_rows = (dot(g_rows, w_second, 1, 1) * slope_rows).astype(BF16)
    sums = [own[:, :width], own[:, width:], to_next0, to_next1, to_prev0, to_prev1]
    *sums, d_rows = lax.optimization_barrier((*sums, d_rows))
    packed, d_rows, g_rows = lax.optimization_barrier((pack(hot, sums), d_rows, g_rows))
    first = dot(x_rows, d_rows).astype(BF16)
    second = dot(h_rows, g_rows).astype(BF16)
    layer_out = final(tgt, mixed, flat(exchange(packed)))
    return (layer_out, first[None], second[None])


def solution(mesh):
    token = P(("dp", "expert"), "seq", None)
    first = P(("seq", "expert"), None, "dp")
    second = P(("seq", "expert"), "dp", None)
    return jax.shard_map(
        shards,
        mesh=mesh,
        in_specs=(token,) * 6 + (P(), first, second),
        out_specs=(token, first, second),
        check_vma=False,
    )
```
